32 devices in a mesh: groups: 2 (over x), dp: 4 (over z), tensor: 4 (over y, core).
Axes of the slice: x: 2, y: 2, z: 4, core: 2. Of those that a mesh axis runs over, the one named last changes fastest.
Arguments:
- tokens: bfloat16 [4096, 8192], P(('groups', 'dp'), 'tensor'), parts along dimension 0, may hold values from -6 to 6
- cotangent: bfloat16 [4096, 8192], P(('groups', 'dp'), 'tensor'), parts along dimension 0, may hold values from -6 to 6
- frozen_weight: bfloat16 [8192, 8192], P('tensor'), may hold values from -0.09375 to 0.09375
- adapter_down_table: bfloat16 [32, 8192, 64], P(('groups', 'dp'), 'tensor'), parts along dimension 0, may hold values from -0.75 to 0.75
- adapter_up_table: bfloat16 [32, 64, 8192], P(('groups', 'dp'), None, 'tensor'), parts along dimension 0, may hold values from -0.75 to 0.75
- segment_adapter_id: int32 [32], P(('groups', 'dp')), parts along dimension 0, may hold values from 0 to 15, as said below
- segment_live_length: int32 [32], P(('groups', 'dp')), parts along dimension 0, may hold values from 1 to 128, as said below
- adapter_table_row: int32 [32], P('groups'), parts along dimension 0, may hold values from 0 to 15, as said below
Outputs:
- layer_result: bfloat16 [4096, 8192], P(('groups', 'dp'), 'tensor'), parts along dimension 0
- token_input_gradient: bfloat16 [4096, 8192], P(('groups', 'dp'), 'tensor'), parts along dimension 0
- down_grad: float32 [32, 8192, 64], P(('groups', 'dp'), 'tensor'), parts along dimension 0
- up_grad: float32 [32, 64, 8192], P(('groups', 'dp'), None, 'tensor'), parts along dimension 0
The draws below stay inside these ranges and needn't reach their ends.
There are 2 independent parts, one for each index of `groups`. The reference program is written for one: setup_inputs(seed, part) draws one part's arguments, and reference() takes and returns one part's arrays. A program takes and returns all parts, laid end to end along the dimension named above; an argument that names none is the same for every part. Nothing has to cross between parts.
Inputs may be any that keep to these rules, and one draw needn't show every extreme that they name: `segment_adapter_id`: the owner of an adapter along dp is adapter_table_row of it // 4. At most 2 segments of one device name adapters of one owner; in every draw some owner has exactly 2 segments of every device. `adapter_table_row`: A permutation of the table rows. `segment_live_length`: some segment is full.
All inputs are finite; a program needn't handle non-finite values.
Results may differ from the reference program's by a relative error of at most 0.013.
Values may be sent and summed in bfloat16 or wider, within the bound.
No kernel may reach another device: no remote copies, remote signals or barrier semaphores. Data moves between devices by JAX's collectives and lax.ppermute only.
A program may use at most 192 MiB of HBM per device.

```python
import jax
import jax.numpy as jnp
from jax import lax

MODEL_WIDTH = 8192
ADAPTER_RANK = 64
SEGLEN = 128
SEG_DEV = 4
ADAPT_DEV = 4
CAP = 2
NSEG = 16
ROW_TOTAL = 2048
ADAPTER_TOTAL = 16


def common_routing(key):
    device_count = NSEG // SEG_DEV
    slot_perm = jax.random.permutation(jax.random.fold_in(key, 11), ADAPTER_TOTAL).astype(jnp.int32)
    hot_owner = jax.random.randint(jax.random.fold_in(key, 12), (), 0, device_count)
    offset = jax.random.randint(jax.random.fold_in(key, 13), (device_count, 1), 0, device_count - 1)
    positions = jnp.arange(SEG_DEV)[None, :]
    spill = jnp.maximum(positions - CAP, 0) // CAP
    others = (hot_owner + 1 + (offset + spill) % (device_count - 1)) % device_count
    owners = jnp.where(positions < CAP, hot_owner, others)
    scores = jax.random.randint(jax.random.fold_in(key, 14), (device_count, SEG_DEV), 0, 1 << 20) * SEG_DEV + positions
    shuffle = jnp.argsort(scores, axis=1)
    owners = jnp.take_along_axis(owners, shuffle, axis=1)
    first_pick = jax.random.randint(jax.random.fold_in(key, 15), (device_count, SEG_DEV), 0, ADAPT_DEV)
    second_pick = jax.random.randint(jax.random.fold_in(key, 16), (device_count, SEG_DEV), 0, ADAPT_DEV)
    local_pick = jnp.minimum(first_pick, second_pick)
    slot_table_rows = (owners * ADAPT_DEV + local_pick).reshape(NSEG)
    inverse = jnp.argsort(slot_perm).astype(jnp.int32)
    adapters = jnp.take(inverse, slot_table_rows).astype(jnp.int32)
    return (slot_perm, adapters)


def draw_adapter_table_row(key, part):
    return common_routing(key)[0]


def draw_segment_adapter_id(key, part):
    return common_routing(key)[1]


def draw_segment_live_length(key, part):
    key = jax.random.fold_in(key, 21)
    lengths = jax.random.randint(jax.random.fold_in(key, 1), (NSEG,), 1, SEGLEN + 1)
    full_index = jax.random.randint(jax.random.fold_in(key, 2), (), 0, NSEG)
    return jnp.where(jnp.arange(NSEG) == full_index, SEGLEN, lengths).astype(jnp.int32)


def spiked(values, rng, source, target, blocks, factor):
    def block_of(dim):
        return (jnp.arange(values.shape[dim]) // (values.shape[dim] // blocks)).reshape((-1,) + (1,) * (values.ndim - 1 - dim))

    near = jax.random.permutation(rng, blocks)[block_of(target)]
    far = (block_of(target) + blocks // 2) % blocks
    return jnp.where((block_of(source) == near) | (block_of(source) == far), factor * values, values)


def level_of(key, extent, cuts, least, top_value):
    loudness = 1.0
    for axis_at, shards_of in cuts:
        heights = jax.random.uniform(jax.random.fold_in(jax.random.fold_in(key, 6), axis_at), (shards_of,), jnp.float32, least / len(cuts), top_value / len(cuts))
        loudness = loudness * jnp.repeat(jnp.exp(heights), extent[axis_at] // shards_of).reshape((-1,) + (1,) * (len(extent) - 1 - axis_at))
    return loudness


def bell_draw(stream_key, dims, spread, reach, pieces=(), held_as=jnp.bfloat16):
    factor_of = level_of(stream_key, dims, pieces, -0.22, 0.18) if pieces else 1.0
    entries = jax.random.normal(stream_key, dims, jnp.float32) * spread * factor_of
    return jnp.minimum(jnp.maximum(entries, -reach), reach).astype(held_as)


def heavy_noise(rng, shape, width, limit, split, heavy, dtype=jnp.bfloat16):
    result = width * jax.random.normal(rng, shape, jnp.float32)
    if split:
        result = result * level_of(rng, shape, split, -0.22, 0.18)
    return jnp.clip(spiked(result, jax.random.fold_in(rng, 3), *heavy), -limit, limit).astype(dtype)


def setup_inputs(seed: int = 0, part: int = 0) -> dict:
    seeds = jax.random.split(jax.random.key(seed), 9)
    part_keys = jax.random.split(jax.random.fold_in(seeds[8], part), 9)
    tokens = bell_draw(part_keys[0], (ROW_TOTAL, MODEL_WIDTH), 1.0, 6.0, ((0, 4), (1, 4)))
    cotangent = bell_draw(part_keys[1], (ROW_TOTAL, MODEL_WIDTH), 1.0, 6.0, ((0, 4), (1, 4)))
    frozen_weight = heavy_noise(seeds[2], (MODEL_WIDTH, MODEL_WIDTH), MODEL_WIDTH ** -0.5, 0.09375, ((0, 4),), (0, 1, 4, 2.0))
    adapter_down_table = bell_draw(part_keys[3], (ADAPTER_TOTAL, MODEL_WIDTH, ADAPTER_RANK), ADAPTER_RANK ** -0.5, 0.75, ((0, 4), (1, 4)))
    adapter_up_table = bell_draw(part_keys[4], (ADAPTER_TOTAL, ADAPTER_RANK, MODEL_WIDTH), ADAPTER_RANK ** -0.5, 0.75, ((0, 4), (2, 4)))
    segment_adapter_id = draw_segment_adapter_id(jax.random.fold_in(jax.random.fold_in(seeds[8], part), 71), part)
    segment_live_length = draw_segment_live_length(jax.random.fold_in(jax.random.fold_in(seeds[8], part), 71), part)
    adapter_table_row = draw_adapter_table_row(jax.random.fold_in(jax.random.fold_in(seeds[8], part), 71), part)
    return dict(tokens=tokens, cotangent=cotangent, frozen_weight=frozen_weight, adapter_down_table=adapter_down_table, adapter_up_table=adapter_up_table, segment_adapter_id=segment_adapter_id, segment_live_length=segment_live_length, adapter_table_row=adapter_table_row)


adapter_scale = 0.015625
highest_precision = lax.Precision.HIGHEST


def reference(tokens, cotangent, frozen_weight, adapter_down_table, adapter_up_table, segment_adapter_id, segment_live_length, adapter_table_row):
    slot_table_rows = jnp.take(adapter_table_row, segment_adapter_id).astype(jnp.int32)
    segment_down_factor = jnp.take(adapter_down_table, slot_table_rows, axis=0).astype(jnp.float32)
    segment_up_factor = jnp.take(adapter_up_table, slot_table_rows, axis=0).astype(jnp.float32)
    live_mask = (jnp.arange(SEGLEN)[None, :] < segment_live_length[:, None]).astype(jnp.float32)[:, :, None]
    tok_seg = tokens.reshape(NSEG, SEGLEN, MODEL_WIDTH).astype(jnp.float32)
    segment_cotangent = cotangent.reshape(NSEG, SEGLEN, MODEL_WIDTH).astype(jnp.float32)
    down_activation = jnp.einsum('ksd,kdr->ksr', tok_seg, segment_down_factor, precision=highest_precision)
    frozen_output = jnp.dot(tokens, frozen_weight, preferred_element_type=jnp.float32)
    adapter_output = jnp.einsum('enu,euz->enz', down_activation, segment_up_factor, precision=highest_precision) * (adapter_scale * live_mask)
    layer_result = (frozen_output + adapter_output.reshape(ROW_TOTAL, MODEL_WIDTH)).astype(jnp.bfloat16)
    output_gradient = jnp.einsum('hln,hcn->hlc', segment_cotangent, segment_up_factor, precision=highest_precision) * (adapter_scale * live_mask)
    frozen_backward = jnp.dot(cotangent, frozen_weight.T, preferred_element_type=jnp.float32)
    adapter_backward = jnp.einsum('omj,oxj->omx', output_gradient, segment_down_factor, precision=highest_precision)
    token_input_gradient = (frozen_backward + adapter_backward.reshape(ROW_TOTAL, MODEL_WIDTH)).astype(jnp.bfloat16)
    down_terms = jnp.einsum('ksd,ksr->kdr', tok_seg, output_gradient, precision=highest_precision).astype(jnp.bfloat16)
    scaled_activation = down_activation * (adapter_scale * live_mask)
    up_terms = jnp.einsum('ksr,ksd->krd', scaled_activation, segment_cotangent, precision=highest_precision).astype(jnp.bfloat16)
    down_terms, up_terms = lax.optimization_barrier((down_terms, up_terms))
    down_grad = jnp.zeros((ADAPTER_TOTAL, MODEL_WIDTH, ADAPTER_RANK), jnp.float32).at[slot_table_rows].add(down_terms.astype(jnp.float32))
    up_grad = jnp.zeros((ADAPTER_TOTAL, ADAPTER_RANK, MODEL_WIDTH), jnp.float32).at[slot_table_rows].add(up_terms.astype(jnp.float32))
    return layer_result, token_input_gradient, down_grad, up_grad
```

```python
import functools

import jax
import jax.numpy as jnp
from jax import lax
from jax.experimental import pallas as pl
from jax.experimental.pallas import tpu as pltpu
from jax.sharding import PartitionSpec as P

SCALE = 0.015625
STEPS = 5
COLS = 128
SEND_R, RECV_R, SEND_L, RECV_L, SRC_R, SRC_L, SRC_SEG, TOTAL = range(8)


def plan_kernel(n_dev, n_own, n_seg, steps, me_ref, rel_ref, plan_ref, far_ref):
    me = me_ref[0]

    def clear(i, carry):
        for row in range(4):
            plan_ref[row, i] = -1
        return carry

    lax.fori_loop(0, COLS, clear, 0)
    total = jnp.int32(0)
    for left in (False, True):
        mirror = (lambda v: n_dev - 1 - v) if left else (lambda v: v)
        send, recv = (SEND_L, RECV_L) if left else (SEND_R, RECV_R)
        for o in range(n_dev):
            for a in range(n_own):
                far_ref[o * n_own + a] = o
        for r in range(n_dev):
            row = lax.rem(me - r + n_dev, n_dev)
            for k in range(n_seg):
                slot = rel_ref[row, k]
                owner = lax.div(slot, n_own)
                item = mirror(owner) * n_own + slot - owner * n_own
                far_ref[item] = jnp.maximum(far_ref[item], mirror(r))
        far = [[far_ref[o * n_own + a] for a in range(n_own)] for o in range(n_dev)]
        place = mirror(me)
        base = {}
        for c in range(n_dev - 1):
            at = jnp.int32(0)
            for o in range(c, -1, -1):
                if o < c:
                    at = jnp.maximum(base[o, c - 1] + 1, at)
                base[o, c] = at
                for f in range(n_dev - 1, c, -1):
                    for a in range(n_own):
                        hit = far[o][a] == f
                        item = mirror(o) * n_own + a
                        plan_ref[send, jnp.where(hit & (place == c), at, COLS - 1)] = item
                        plan_ref[recv, jnp.where(hit & (place == c + 1), at, COLS - 1)] = item
                        at = at + hit.astype(jnp.int32)
            total = jnp.maximum(total, at)
    plan_ref[TOTAL, 0] = total
    got_r = [plan_ref[RECV_R, t] for t in range(steps)]
    got_l = [plan_ref[RECV_L, t] for t in range(steps)]

    def find(item, r_count, l_count):
        owner = lax.div(item, n_own)
        at = jnp.where(owner == me, item - owner * n_own, 0)
        for t in range(r_count):
            at = jnp.where(got_r[t] == item, n_own + t, at)
        for t in range(l_count):
            at = jnp.where(got_l[t] == item, n_own + steps + t, at)
        return at

    for t in range(steps):
        item = plan_ref[SEND_R, t]
        plan_ref[SRC_R, t] = jnp.where(item >= 0, find(jnp.maximum(item, 0), t, 0), 0)
        item = plan_ref[SEND_L, t]
        plan_ref[SRC_L, t] = jnp.where(item >= 0, find(jnp.maximum(item, 0), 0, t), 0)
    for k in range(n_seg):
        plan_ref[SRC_SEG, k] = find(rel_ref[0, k], steps, steps)


def make_plan(me, relative, n_own):
    n_dev, n_seg = relative.shape
    smem = pl.BlockSpec(memory_space=pltpu.SMEM)
    return pl.pallas_call(
        functools.partial(plan_kernel, n_dev, n_own, n_seg, STEPS),
        out_shape=jax.ShapeDtypeStruct((8, COLS), jnp.int32),
        in_specs=[smem, smem],
        out_specs=smem,
        scratch_shapes=[pltpu.SMEM((n_dev * n_own,), jnp.int32)],
        name="plan",
    )(me.reshape(1), relative)


def pick_kernel(row, cols, slots, plan_ref, table_ref, *rest):
    blocks, out_ref, sem = rest[:-2], rest[-2], rest[-1]
    n_own = table_ref.shape[0]
    for i, c in enumerate(cols):
        at = plan_ref[row, c]

        @pl.when(at < n_own)
        def _(i=i, at=at):
            pltpu.make_async_copy(table_ref.at[at], out_ref.at[i], sem.at[i]).start()

        for ref, slot in zip(blocks, slots):

            @pl.when(at == slot)
            def _(i=i, ref=ref):
                pltpu.make_async_copy(ref, out_ref.at[i], sem.at[i]).start()

    for i in range(len(cols)):
        pltpu.make_async_copy(table_ref.at[0], out_ref.at[i], sem.at[i]).wait()


def pick(plan, row, cols, table, blocks, slots):
    anywhere = pl.BlockSpec(memory_space=pl.ANY)
    return pl.pallas_call(
        functools.partial(pick_kernel, row, tuple(cols), tuple(slots)),
        out_shape=jax.ShapeDtypeStruct((len(cols),) + table.shape[1:], table.dtype),
        in_specs=[pl.BlockSpec(memory_space=pltpu.SMEM)] + [anywhere] * (1 + len(blocks)),
        out_specs=anywhere,
        scratch_shapes=[pltpu.SemaphoreType.DMA((len(cols),))],
        name="pick",
    )(plan, table, *blocks)


def chosen(pairs):
    total = None
    for mask, block in pairs:
        term = jnp.where(mask, block.astype(jnp.float32), 0.0)
        total = term if total is None else total + term
    return total


def body(
    tokens,
    cotangent,
    weight,
    down_table,
    up_table,
    segment_adapter_id,
    segment_live_length,
    adapter_table_row,
):
    n_seg = segment_adapter_id.shape[0]
    rows, width = tokens.shape
    seg_rows = rows // n_seg
    n_own, _, rank = down_table.shape
    n_dev = lax.axis_size("dp")
    n_groups = lax.axis_size("groups")
    n_tensor = lax.axis_size("tensor")
    n_chips = n_tensor // 2
    me_dev = lax.axis_index("dp")
    me = lax.axis_index("tensor")
    chip, core = me // 2, me % 2
    f32, bf16 = jnp.float32, jnp.bfloat16

    to_core = [(i, i ^ 1) for i in range(n_tensor)]

    def to_chip(s):
        return [(i, (i // 2 + s) % n_chips * 2 + i % 2) for i in range(n_tensor)]

    rightward = [(i, i + 1) for i in range(n_dev - 1)]
    leftward = [(i + 1, i) for i in range(n_dev - 1)]

    one = segment_adapter_id[:, None] == jnp.arange(adapter_table_row.shape[0])[None, :]
    slots = jnp.sum(jnp.where(one, adapter_table_row[None, :], 0), axis=1).astype(jnp.int32)
    relative = [slots]
    for s in range(1, n_dev):
        relative.append(lax.ppermute(slots, "dp", [(i, (i + s) % n_dev) for i in range(n_dev)]))
    plan = make_plan(me_dev.astype(jnp.int32), jnp.stack(relative), n_own)
    most = plan[TOTAL, 0]
    for s in range(1, n_groups):
        other = lax.ppermute(
            plan[TOTAL, :1], "groups", [(i, (i + s) % n_groups) for i in range(n_groups)]
        )
        most = jnp.maximum(most, other[0])
    long_way = most > STEPS

    blocks = [(me, cotangent), (me ^ 1, lax.ppermute(cotangent, "tensor", to_core))]
    for s in range(1, n_chips):
        far = lax.ppermute(cotangent, "tensor", to_chip(s))
        owner = (chip - s) % n_chips * 2 + core
        blocks.append((owner, far))
        blocks.append((owner ^ 1, lax.ppermute(far, "tensor", to_core)))

    down_t = jnp.swapaxes(down_table, 1, 2)

    def hops(table):
        got_r, got_l = [], []
        for t in range(STEPS):
            send = pick(plan, SRC_R, [t], table, got_r, [n_own + i for i in range(t)])[0]
            got_r.append(lax.ppermute(send, "dp", rightward))
            send = pick(plan, SRC_L, [t], table, got_l, [n_own + STEPS + i for i in range(t)])[0]
            got_l.append(lax.ppermute(send, "dp", leftward))
        return pick(
            plan,
            SRC_SEG,
            range(n_seg),
            table,
            got_r + got_l,
            [n_own + i for i in range(2 * STEPS)],
        )

    down_seg, up_seg = hops(down_t), hops(up_table)

    capacity = max(2, n_seg // 2)
    owners, local = slots // n_own, slots % n_own
    before = jnp.arange(n_seg)[None, :] < jnp.arange(n_seg)[:, None]
    order = jnp.sum(jnp.logical_and(owners[:, None] == owners[None, :], before), axis=1)
    placement = owners * capacity + order
    placed = placement[:, None] == jnp.arange(n_dev * capacity)[None, :]

    def swap(x):
        x = x.reshape((n_dev, capacity) + x.shape[1:])
        x = lax.all_to_all(x, "dp", split_axis=0, concat_axis=0, tiled=True)
        return x.reshape((n_dev * capacity,) + x.shape[2:])

    def requests():
        asked = jnp.sum(jnp.where(placed, local[:, None] + 1, 0), axis=0) - 1
        return swap(asked)

    def fetch(down_seg, up_seg):
        at = jnp.maximum(requests(), 0)
        return tuple(
            jnp.take(swap(jnp.take(t, at, axis=0)), placement, axis=0) for t in (down_t, up_table)
        )

    down_seg, up_seg = lax.cond(long_way, fetch, lambda a, b: (a, b), down_seg, up_seg)

    tok_seg = tokens.reshape(n_seg, seg_rows, width)
    cot_seg = cotangent.reshape(n_seg, seg_rows, width)
    live = jnp.arange(seg_rows)[None, :] < segment_live_length[:, None]
    live = jnp.where(live, SCALE, 0.0).astype(f32)[:, None, :]

    def summed(part):
        part = part + lax.ppermute(part, "tensor", to_core)
        total = part
        for s in range(1, n_chips):
            total = total + lax.ppermute(part, "tensor", to_chip(s))
        return total

    def low_rank(factor, acts):
        return jnp.einsum("krd,ksd->krs", factor, acts, preferred_element_type=f32)

    act = (summed(low_rank(down_seg, tok_seg)) * live).astype(bf16)
    up_terms = jnp.einsum("krs,ksd->krd", act, cot_seg, preferred_element_type=f32).astype(bf16)
    grad = (summed(low_rank(up_seg, cot_seg)) * live).astype(bf16)
    down_terms = jnp.einsum("krs,ksd->krd", grad, tok_seg, preferred_element_type=f32).astype(bf16)

    def items(row):
        return [plan[row, t] for t in range(STEPS)]

    send_r, recv_r, send_l, recv_l = (items(r) for r in (SEND_R, RECV_R, SEND_L, RECV_L))

    def hops_back(terms):
        own = [(slots[k], terms[k]) for k in range(n_seg)]
        from_r, from_l = [], []
        for t in range(STEPS - 1, -1, -1):
            send = chosen([(i == recv_r[t], b) for i, b in own + from_r]).astype(bf16)
            new_r = (send_r[t], lax.ppermute(send, "dp", leftward))
            send = chosen([(i == recv_l[t], b) for i, b in own + from_l]).astype(bf16)
            new_l = (send_l[t], lax.ppermute(send, "dp", rightward))
            from_r.append(new_r)
            from_l.append(new_l)
        return jnp.stack(
            [
                chosen([(i == me_dev * n_own + j, b) for i, b in own + from_r + from_l])
                for j in range(n_own)
            ]
        )

    up_grad, down_grad = hops_back(up_terms), hops_back(down_terms)

    def give(up_grad, down_grad):
        asked = requests()
        select = (asked[None, :] == jnp.arange(n_own)[:, None]).astype(bf16)

        def back(terms):
            sent = jnp.zeros((n_dev * capacity,) + terms.shape[1:], bf16).at[placement].set(terms)
            return jnp.einsum("os,srd->ord", select, swap(sent), preferred_element_type=f32)

        return back(up_terms), back(down_terms)

    up_grad, down_grad = lax.cond(long_way, give, lambda a, b: (a, b), up_grad, down_grad)

    def columns(owner):
        return lax.dynamic_slice_in_dim(weight, owner * width, width, axis=1)

    def partial(owner):
        return jnp.dot(tokens, columns(owner), preferred_element_type=f32)

    pieces = []
    for s in range(1, n_chips):
        owner = (chip + s) % n_chips * 2 + core
        met = lax.ppermute(partial(owner ^ 1).astype(bf16), "tensor", to_core)
        pair = (partial(owner) + met.astype(f32)).astype(bf16)
        pieces.append(lax.ppermute(pair, "tensor", to_chip(s)))
    met = lax.ppermute(partial(me ^ 1).astype(bf16), "tensor", to_core)
    total = partial(me) + met.astype(f32)
    for piece in pieces:
        total = total + piece.astype(f32)
    added = jnp.einsum("krs,krd->ksd", act, up_seg, preferred_element_type=f32)
    layer_result = (total + added.reshape(rows, width)).astype(bf16)

    back = jnp.einsum("krs,krd->ksd", grad, down_seg, preferred_element_type=f32)
    back = back.reshape(rows, width)
    for owner, block in blocks:
        back = back + lax.dot_general(
            block, columns(owner), (((1,), (1,)), ((), ())), preferred_element_type=f32
        )
    return layer_result, back.astype(bf16), jnp.swapaxes(down_grad, 1, 2), up_grad


def solution(mesh):
    placed = (
        P(("groups", "dp"), "tensor"),
        P(("groups", "dp"), "tensor"),
        P("tensor", None),
        P(("groups", "dp"), "tensor", None),
        P(("groups", "dp"), None, "tensor"),
        P(("groups", "dp")),
        P(("groups", "dp")),
        P("groups"),
    )
    return jax.shard_map(
        body,
        mesh=mesh,
        in_specs=placed,
        out_specs=(
            P(("groups", "dp"), "tensor"),
            P(("groups", "dp"), "tensor"),
            P(("groups", "dp"), "tensor", None),
            P(("groups", "dp"), None, "tensor"),
        ),
        check_vma=False,
    )
```

```python
import functools

import jax
import jax.numpy as jnp
from jax import lax
from jax.experimental import pallas as pl
from jax.experimental.pallas import tpu as pltpu
from jax.sharding import PartitionSpec as P

SCALE = 0.015625
STEPS = 6
LAG = 2
COLS = 128
SEND_R, RECV_R, SEND_L, RECV_L, SRC_R, SRC_L, SRC_SEG, MISC = range(8)
SHORT, ME = 64, 65
F32, BF16 = jnp.float32, jnp.bfloat16
SMEM = pl.BlockSpec(memory_space=pltpu.SMEM)
VMEM = pl.BlockSpec(memory_space=pltpu.VMEM)
ANYWHERE = pl.BlockSpec(memory_space=pl.ANY)
PARAMS = pltpu.CompilerParams(vmem_limit_bytes=36 << 20)


def cost(flops, nbytes):
    return pl.CostEstimate(flops=flops, bytes_accessed=nbytes, transcendentals=0)


def plan_kernel(n_dev, n_own, n_seg, me_ref, rel_ref, plan_ref, far_ref):
    me = me_ref[0]
    short = jnp.int32(0)
    table = {}
    for left in (False, True):
        mirror = (lambda v: n_dev - 1 - v) if left else (lambda v: v)
        for o in range(n_dev):
            for a in range(n_own):
                far_ref[o * n_own + a] = o
        for r in range(n_dev):
            row = lax.rem(me - r + n_dev, n_dev)
            for k in range(n_seg):
                slot = rel_ref[row, k]
                owner = lax.div(slot, n_own)
                item = mirror(owner) * n_own + slot - owner * n_own
                far_ref[item] = jnp.maximum(far_ref[item], mirror(r))
        n_items = n_dev * n_own
        far = [far_ref[i] for i in range(n_items)]
        at = [jnp.int32(i // n_own) for i in range(n_items)]
        ready = [jnp.int32(0) for i in range(n_items)]
        place = mirror(me)
        for t in range(STEPS):
            send, recv = jnp.int32(-1), jnp.int32(-1)
            best = []
            for d in range(n_dev - 1):
                key = jnp.int32(-1)
                for i in range((d + 1) * n_own):
                    if i // n_own < d and LAG * (d - i // n_own) > t:
                        continue
                    can = (at[i] == d) & (far[i] > d) & (ready[i] <= t)
                    key = jnp.maximum(key, jnp.where(can, far[i] * n_items + i, -1))
                best.append(key)
            for d in range(n_dev - 1):
                item = lax.rem(best[d], n_items)
                for i in range((d + 1) * n_own):
                    hit = (best[d] >= 0) & (item == i)
                    at[i] = jnp.where(hit, d + 1, at[i])
                    ready[i] = jnp.where(hit, t + LAG, ready[i])
                owner = lax.div(item, n_own)
                name = mirror(owner) * n_own + item - owner * n_own
                name = jnp.where(best[d] >= 0, name, -1)
                send = jnp.where(place == d, name, send)
                recv = jnp.where(place == d + 1, name, recv)
            table[left, t] = (send, recv)
            plan_ref[SEND_L if left else SEND_R, t] = send
            plan_ref[RECV_L if left else RECV_R, t] = recv
        for i in range(n_items):
            short = short + (at[i] < far[i]).astype(jnp.int32)

    def find(item, r_count, l_count):
        owner = lax.div(item, n_own)
        at = jnp.where(owner == me, item - owner * n_own, 0)
        for t in range(r_count):
            at = jnp.where(table[False, t][1] == item, n_own + t, at)
        for t in range(l_count):
            at = jnp.where(table[True, t][1] == item, n_own + STEPS + t, at)
        return at

    for t in range(STEPS):
        known = max(0, t - LAG + 1)
        item = table[False, t][0]
        plan_ref[SRC_R, t] = jnp.where(item >= 0, find(jnp.maximum(item, 0), known, 0), 0)
        item = table[True, t][0]
        plan_ref[SRC_L, t] = jnp.where(item >= 0, find(jnp.maximum(item, 0), 0, known), 0)
    for k in range(n_seg):
        slot = rel_ref[0, k]
        plan_ref[SRC_SEG, k] = find(slot, STEPS, STEPS)
        plan_ref[MISC, k] = slot
    plan_ref[MISC, SHORT] = short
    plan_ref[MISC, ME] = me


def make_plan(me, relative, n_own):
    n_dev, n_seg = relative.shape
    return pl.pallas_call(
        functools.partial(plan_kernel, n_dev, n_own, n_seg),
        out_shape=jax.ShapeDtypeStruct((8, COLS), jnp.int32),
        in_specs=[SMEM, SMEM],
        out_specs=SMEM,
        scratch_shapes=[pltpu.SMEM((n_dev * n_own,), jnp.int32)],
        name="plan",
    )(me.reshape(1), relative)


def pick_kernel(wanted, slots, plan_ref, table_ref, *rest):
    n_out = len(wanted)
    blocks, outs, sem = rest[: -n_out - 1], rest[-n_out - 1 : -1], rest[-1]
    n_own = table_ref.shape[0]
    places = [(outs[o], row, c, i) for o, (row, cols) in enumerate(wanted) for i, c in enumerate(cols)]
    for n, (out, row, c, i) in enumerate(places):
        at = plan_ref[row, c]

        @pl.when(at < n_own)
        def _(out=out, i=i, at=at, n=n):
            pltpu.make_async_copy(table_ref.at[at], out.at[i], sem.at[n]).start()

        for ref, slot in zip(blocks, slots):

            @pl.when(at == slot)
            def _(out=out, i=i, ref=ref, n=n):
                pltpu.make_async_copy(ref, out.at[i], sem.at[n]).start()

    for n, (out, row, c, i) in enumerate(places):
        pltpu.make_async_copy(table_ref.at[0], out.at[i], sem.at[n]).wait()


def pick(plan, wanted, table, blocks, slots):
    shape = table.shape[1:]
    count = sum(len(cols) for _, cols in wanted)
    size = count * shape[0] * shape[1]
    return pl.pallas_call(
        functools.partial(pick_kernel, wanted, tuple(slots)),
        out_shape=[jax.ShapeDtypeStruct((len(cols),) + shape, table.dtype) for _, cols in wanted],
        in_specs=[SMEM] + [ANYWHERE] * (1 + len(blocks)),
        out_specs=[VMEM] * len(wanted),
        scratch_shapes=[pltpu.SemaphoreType.DMA((count,))],
        cost_estimate=cost(0, 4 * size),
        compiler_params=PARAMS,
        name="pick",
    )(plan, table, *blocks)


def gather_sum(plan_ref, item, terms_ref, keyed, acc, held, sem):
    acc[...] = jnp.zeros_like(acc)
    for k in range(terms_ref.shape[0]):

        @pl.when(plan_ref[MISC, k] == item)
        def _(k=k):
            acc[...] += terms_ref[k].astype(F32)

    for ref, (row, t) in keyed:

        @pl.when(plan_ref[row, t] == item)
        def _(ref=ref):
            copy = pltpu.make_async_copy(ref, held, sem)
            copy.start()
            copy.wait()
            acc[...] += held[...].astype(F32)


def back_kernel(t, keys, plan_ref, terms_ref, *rest):
    blocks = rest[: len(keys)]
    to_left, to_right, acc, held, sem = rest[len(keys) :]
    keyed = list(zip(blocks, keys))
    for out, row, side in ((to_left, RECV_R, SEND_R), (to_right, RECV_L, SEND_L)):
        mine = [(b, k) for b, k in keyed if k[0] == side]
        gather_sum(plan_ref, plan_ref[row, t], terms_ref, mine, acc, held, sem)
        out[...] = acc[...].astype(out.dtype)


def final_kernel(n_own, keys, plan_ref, terms_ref, *rest):
    blocks = rest[: len(keys)]
    down_ref, up_ref, acc, held, sem = rest[len(keys) :]
    item = plan_ref[MISC, ME] * n_own + pl.program_id(0)
    gather_sum(plan_ref, item, terms_ref, list(zip(blocks, keys)), acc, held, sem)
    rank = acc.shape[0] // 2
    down_ref[0] = acc[:rank]
    up_ref[0] = acc[rank:]


def low_rank_kernel(factor_ref, tok_ref, cot_ref, out_ref):
    rank = factor_ref.shape[1] // 2
    for half, act in ((0, tok_ref), (1, cot_ref)):
        rows = slice(half * rank, (half + 1) * rank)
        out_ref[0, rows] = lax.dot_general(
            factor_ref[0, rows], act[...], (((1,), (1,)), ((), ())), preferred_element_type=F32
        )


def terms_kernel(live_ref, total_ref, tok_ref, cot_ref, act_ref, terms_ref):
    rank = total_ref.shape[1] // 2
    total = total_ref[0]
    column = lax.broadcasted_iota(jnp.int32, total.shape, 1)
    act = jnp.where(column < live_ref[pl.program_id(0)], total * SCALE, 0.0).astype(BF16)
    act_ref[0] = act
    for rows, left, right in (
        (slice(0, rank), act[rank:], tok_ref),
        (slice(rank, 2 * rank), act[:rank], cot_ref),
    ):
        terms_ref[0, rows] = jnp.dot(left, right[...], preferred_element_type=F32).astype(BF16)


def forward_kernel(n_extra, low_rank, owner_ref, x_ref, w_ref, *rest):
    out_ref = rest[-1]
    out = jnp.dot(x_ref[...], w_ref[...], preferred_element_type=F32)
    for extra in rest[:n_extra]:
        out = out + extra[...].astype(F32)
    if low_rank:
        add_low_rank(out, rest[n_extra], rest[n_extra + 1], out_ref)
    else:
        out_ref[...] = out.astype(out_ref.dtype)


def add_low_rank(out, act_ref, factor_ref, out_ref):
    n_seg, _, seg_rows = act_ref.shape
    for k in range(n_seg):
        rows = slice(k * seg_rows, (k + 1) * seg_rows)
        term = lax.dot_general(
            act_ref[k], factor_ref[k], (((0,), (0,)), ((), ())), preferred_element_type=F32
        )
        out_ref[rows] = (out[rows] + term).astype(out_ref.dtype)


def forward(owner, x, weight, extras=(), low_rank=None, dtype=BF16):
    rows, width = x.shape
    block = min(512, width)
    per = width // block
    here = pl.BlockSpec((rows, block), lambda j, o: (0, j))
    in_specs = [
        pl.BlockSpec((rows, width), lambda j, o: (0, 0)),
        pl.BlockSpec((width, block), lambda j, o: (0, o[0] * per + j)),
    ] + [here] * len(extras)
    args = [x, weight, *extras]
    if low_rank is not None:
        act, factor = low_rank
        n_seg, both, seg_rows = act.shape
        in_specs.append(pl.BlockSpec((n_seg, both // 2, seg_rows), lambda j, o: (0, 0, 0)))
        in_specs.append(pl.BlockSpec((n_seg, both // 2, block), lambda j, o: (0, 1, j)))
        args += [act, factor]
    return pl.pallas_call(
        functools.partial(forward_kernel, len(extras), low_rank is not None),
        out_shape=jax.ShapeDtypeStruct((rows, width), dtype),
        grid_spec=pltpu.PrefetchScalarGridSpec(
            num_scalar_prefetch=1, grid=(per,), in_specs=in_specs, out_specs=here
        ),
        cost_estimate=cost(2 * rows * width * width, 2 * width * (width + 2 * rows)),
        compiler_params=PARAMS,
        name="forward",
    )(owner.reshape(1), *args)


def backward_kernel(n, has_acc, low_rank, owner_ref, *rest):
    out_ref = rest[-1]
    out = None
    for x_ref, w_ref in zip(rest[:n], rest[n : 2 * n]):
        term = lax.dot_general(
            x_ref[...], w_ref[...], (((1,), (1,)), ((), ())), preferred_element_type=F32
        )
        out = term if out is None else out + term
    if has_acc:
        out = out + rest[2 * n][...]
    if low_rank:
        add_low_rank(out, rest[2 * n + has_acc], rest[2 * n + has_acc + 1], out_ref)
    else:
        out_ref[...] = out.astype(out_ref.dtype)


def backward(blocks, weight, acc=None, low_rank=None, dtype=F32):
    n = len(blocks)
    rows, width = blocks[0][1].shape
    tile = min(256, width)
    here = pl.BlockSpec((rows, tile), lambda j, o: (0, j))
    in_specs = [pl.BlockSpec((rows, width), lambda j, o: (0, 0))] * n
    in_specs += [pl.BlockSpec((tile, width), lambda j, o, i=i: (j, o[i])) for i in range(n)]
    args = [b for _, b in blocks] + [weight] * n
    if acc is not None:
        in_specs.append(here)
        args.append(acc)
    if low_rank is not None:
        act, factor = low_rank
        n_seg, both, seg_rows = act.shape
        in_specs.append(pl.BlockSpec((n_seg, both // 2, seg_rows), lambda j, o: (0, 1, 0)))
        in_specs.append(pl.BlockSpec((n_seg, both // 2, tile), lambda j, o: (0, 0, j)))
        args += [act, factor]
    return pl.pallas_call(
        functools.partial(backward_kernel, n, int(acc is not None), low_rank is not None),
        out_shape=jax.ShapeDtypeStruct((rows, width), dtype),
        grid_spec=pltpu.PrefetchScalarGridSpec(
            num_scalar_prefetch=1, grid=(width // tile,), in_specs=in_specs, out_specs=here
        ),
        cost_estimate=cost(2 * n * rows * width * width, 2 * n * width * (width + 2 * rows)),
        compiler_params=PARAMS,
        name="backward",
    )(jnp.stack([o for o, _ in blocks]), *args)


def body(
    tokens,
    cotangent,
    weight,
    down_table,
    up_table,
    segment_adapter_id,
    segment_live_length,
    adapter_table_row,
):
    n_seg = segment_adapter_id.shape[0]
    rows, width = tokens.shape
    seg_rows = rows // n_seg
    n_own, _, rank = down_table.shape
    n_dev = lax.axis_size("dp")
    n_groups = lax.axis_size("groups")
    n_tensor = lax.axis_size("tensor")
    n_chips = n_tensor // 2
    me_dev = lax.axis_index("dp").astype(jnp.int32)
    me = lax.axis_index("tensor").astype(jnp.int32)
    chip, core = me // 2, me % 2

    to_core = [(i, i ^ 1) for i in range(n_tensor)]

    def to_chip(s):
        return [(i, (i // 2 + s) % n_chips * 2 + i % 2) for i in range(n_tensor)]

    rightward = [(i, i + 1) for i in range(n_dev - 1)]
    leftward = [(i + 1, i) for i in range(n_dev - 1)]

    one = segment_adapter_id[:, None] == jnp.arange(adapter_table_row.shape[0])[None, :]
    slots = jnp.sum(jnp.where(one, adapter_table_row[None, :], 0), axis=1).astype(jnp.int32)
    relative = [slots]
    for s in range(1, n_dev):
        relative.append(lax.ppermute(slots, "dp", [(i, (i + s) % n_dev) for i in range(n_dev)]))
    plan = make_plan(me_dev, jnp.stack(relative), n_own)

    near = [(me, cotangent), (me ^ 1, lax.ppermute(cotangent, "tensor", to_core))]
    far = []
    for s in range(1, n_chips):
        block = lax.ppermute(cotangent, "tensor", to_chip(s))
        owner = (chip - s) % n_chips * 2 + core
        far.append((owner, block))

    pieces = []
    for s in range(1, n_chips):
        owner = (chip + s) % n_chips * 2 + core
        met = lax.ppermute(forward(owner ^ 1, tokens, weight), "tensor", to_core)
        pair = forward(owner, tokens, weight, (met,))
        pieces.append(lax.ppermute(pair, "tensor", to_chip(s)))
    pieces.append(lax.ppermute(forward(me ^ 1, tokens, weight), "tensor", to_core))

    table = jnp.concatenate([jnp.swapaxes(down_table, 1, 2), up_table], axis=1)
    got_r, got_l = [], []
    for t in range(STEPS):
        known = max(0, t - LAG + 1)
        send_r, send_l = pick(
            plan,
            ((SRC_R, (t,)), (SRC_L, (t,))),
            table,
            got_r[:known] + got_l[:known],
            [n_own + i for i in range(known)] + [n_own + STEPS + i for i in range(known)],
        )
        got_r.append(lax.ppermute(send_r[0], "dp", rightward))
        got_l.append(lax.ppermute(send_l[0], "dp", leftward))
    factors = pick(
        plan,
        ((SRC_SEG, tuple(range(n_seg))),),
        table,
        got_r + got_l,
        [n_own + i for i in range(2 * STEPS)],
    )[0]

    short = plan[MISC, SHORT : SHORT + 1]
    for s in range(1, n_groups):
        pairs = [(i, (i + s) % n_groups) for i in range(n_groups)]
        short = jnp.maximum(short, lax.ppermute(short, "groups", pairs))
    long_way = short[0] > 0

    capacity = max(2, n_seg // 2)

    def places():
        owners = slots // n_own
        before = jnp.arange(n_seg)[None, :] < jnp.arange(n_seg)[:, None]
        order = jnp.sum(jnp.logical_and(owners[:, None] == owners[None, :], before), axis=1)
        return owners * capacity + order

    def swap(x):
        x = x.reshape((n_dev, capacity) + x.shape[1:])
        x = lax.all_to_all(x, "dp", split_axis=0, concat_axis=0, tiled=True)
        return x.reshape((n_dev * capacity,) + x.shape[2:])

    def requests():
        placed = places()[:, None] == jnp.arange(n_dev * capacity)[None, :]
        return swap(jnp.sum(jnp.where(placed, slots[:, None] % n_own + 1, 0), axis=0) - 1)

    def fetch(factors):
        sent = jnp.take(table, jnp.maximum(requests(), 0), axis=0)
        return jnp.take(swap(sent), places(), axis=0)

    factors = lax.cond(long_way, fetch, lambda f: f, factors)
    if far:
        crossed, factors = lax.optimization_barrier(([b for _, b in far], factors))
        far = [(o, b) for (o, _), b in zip(far, crossed)]
        far += [(o ^ 1, lax.ppermute(b, "tensor", to_core)) for o, b in far]

    act_block = pl.BlockSpec((seg_rows, width), lambda k, *_: (k, 0))
    small = pl.BlockSpec((1, 2 * rank, seg_rows), lambda k, *_: (k, 0, 0))
    wide = pl.BlockSpec((1, 2 * rank, width), lambda k, *_: (k, 0, 0))
    part = pl.pallas_call(
        low_rank_kernel,
        out_shape=jax.ShapeDtypeStruct((n_seg, 2 * rank, seg_rows), F32),
        grid=(n_seg,),
        in_specs=[wide, act_block, act_block],
        out_specs=small,
        cost_estimate=cost(4 * rows * width * rank, 6 * rows * width),
        compiler_params=PARAMS,
        name="low_rank",
    )(factors, tokens, cotangent)
    part = part + lax.ppermute(part.astype(BF16), "tensor", to_core).astype(F32)
    total = part
    for s in range(1, n_chips):
        total = total + lax.ppermute(part.astype(BF16), "tensor", to_chip(s)).astype(F32)
    act, terms = pl.pallas_call(
        terms_kernel,
        out_shape=[
            jax.ShapeDtypeStruct((n_seg, 2 * rank, seg_rows), BF16),
            jax.ShapeDtypeStruct((n_seg, 2 * rank, width), BF16),
        ],
        grid_spec=pltpu.PrefetchScalarGridSpec(
            num_scalar_prefetch=1,
            grid=(n_seg,),
            in_specs=[small, act_block, act_block],
            out_specs=[small, wide],
        ),
        cost_estimate=cost(4 * rows * width * rank, 6 * rows * width),
        compiler_params=PARAMS,
        name="terms",
    )(segment_live_length, total, tokens, cotangent)

    block = jax.ShapeDtypeStruct((2 * rank, width), BF16)
    sums = [
        pltpu.VMEM((2 * rank, width), F32),
        pltpu.VMEM((2 * rank, width), BF16),
        pltpu.SemaphoreType.DMA,
    ]
    keys, got = [], []
    for t in range(STEPS - 1, -1, -1):
        known = [i for i, (_, at) in enumerate(keys) if at - t >= LAG]
        to_left, to_right = pl.pallas_call(
            functools.partial(back_kernel, t, tuple(keys[i] for i in known)),
            out_shape=[block, block],
            in_specs=[SMEM, VMEM] + [ANYWHERE] * len(known),
            out_specs=[VMEM, VMEM],
            scratch_shapes=sums,
            cost_estimate=cost(0, 6 * rank * n_seg * width),
            compiler_params=PARAMS,
            name="back",
        )(plan, terms, *[got[i] for i in known])
        got.append(lax.ppermute(to_left, "dp", leftward))
        got.append(lax.ppermute(to_right, "dp", rightward))
        keys += [(SEND_R, t), (SEND_L, t)]
    mine = pl.BlockSpec((1, rank, width), lambda j: (j, 0, 0))
    grad = jax.ShapeDtypeStruct((n_own, rank, width), F32)
    down_grad, up_grad = pl.pallas_call(
        functools.partial(final_kernel, n_own, tuple(keys)),
        out_shape=[grad, grad],
        grid=(n_own,),
        in_specs=[SMEM, pl.BlockSpec((n_seg, 2 * rank, width), lambda j: (0, 0, 0))]
        + [ANYWHERE] * len(got),
        out_specs=[mine, mine],
        scratch_shapes=sums,
        cost_estimate=cost(0, 12 * rank * n_own * width),
        compiler_params=PARAMS,
        name="final",
    )(plan, terms, *got)

    def give(down_grad, up_grad):
        select = (requests()[None, :] == jnp.arange(n_own)[:, None]).astype(BF16)
        sent = jnp.zeros((n_dev * capacity,) + terms.shape[1:], BF16).at[places()].set(terms)
        total = jnp.einsum("os,srd->ord", select, swap(sent), preferred_element_type=F32)
        return total[:, :rank], total[:, rank:]

    down_grad, up_grad = lax.cond(long_way, give, lambda a, b: (a, b), down_grad, up_grad)

    acc = backward(near, weight)
    token_input_gradient = backward(far, weight, acc, (act, factors), BF16)
    layer_result = forward(me, tokens, weight, pieces, (act, factors))
    return layer_result, token_input_gradient, jnp.swapaxes(down_grad, 1, 2), up_grad


def solution(mesh):
    placed = (
        P(("groups", "dp"), "tensor"),
        P(("groups", "dp"), "tensor"),
        P("tensor", None),
        P(("groups", "dp"), "tensor", None),
        P(("groups", "dp"), None, "tensor"),
        P(("groups", "dp")),
        P(("groups", "dp")),
        P("groups"),
    )
    return jax.shard_map(
        body,
        mesh=mesh,
        in_specs=placed,
        out_specs=(
            P(("groups", "dp"), "tensor"),
            P(("groups", "dp"), "tensor"),
            P(("groups", "dp"), "tensor", None),
            P(("groups", "dp"), None, "tensor"),
        ),
        check_vma=False,
    )
```

```python
import functools

import jax
import jax.numpy as jnp
from jax import lax
from jax.experimental import pallas as pl
from jax.experimental.pallas import tpu as pltpu
from jax.sharding import PartitionSpec as P

SCALE = 0.015625
COLS = 128
TILE = 512
SEND, SOURCE, TERM, GIVEN, OWN = range(5)
F32, BF16 = jnp.float32, jnp.bfloat16
SMEM = pl.BlockSpec(memory_space=pltpu.SMEM)
VMEM = pl.BlockSpec(memory_space=pltpu.VMEM)
ANYWHERE = pl.BlockSpec(memory_space=pl.ANY)
HBM = pl.BlockSpec(memory_space=pltpu.HBM)
PARAMS = pltpu.CompilerParams(vmem_limit_bytes=56 << 20)


def cost(flops, nbytes):
    return pl.CostEstimate(flops=flops, bytes_accessed=nbytes, transcendentals=0)


def call(kernel, args, in_specs, after=(), scalars=0, grid=(), out_specs=None, scratch=(), **rest):
    n_in = len(args)

    def body(*refs):
        kernel(*refs[:n_in], *refs[n_in + len(after) :])

    return pl.pallas_call(
        body,
        grid_spec=pltpu.PrefetchScalarGridSpec(
            num_scalar_prefetch=scalars,
            grid=grid,
            in_specs=list(in_specs) + [ANYWHERE] * len(after),
            out_specs=out_specs,
            scratch_shapes=list(scratch),
        ),
        compiler_params=PARAMS,
        **rest,
    )(*args, *after)


def copy_rows(rows, table_ref, outs, held, sem):
    capacity = outs[0].shape[0]
    reads = [
        pltpu.make_async_copy(table_ref.at[row], held.at[c], sem.at[0, c])
        for c, row in enumerate(rows)
    ]
    writes = [
        pltpu.make_async_copy(held.at[c], outs[c // capacity].at[c % capacity], sem.at[1, c])
        for c in range(len(rows))
    ]
    for read in reads:
        read.start()
    for read, write in zip(reads, writes):
        read.wait()
        write.start()
    for write in writes:
        write.wait()


def copies_of(table, count):
    return [
        pltpu.VMEM((count,) + table.shape[1:], table.dtype),
        pltpu.SemaphoreType.DMA((2, count)),
    ]


def request_kernel(capacity, me_ref, rel_ref, table_ref, *rest):
    outs, (plan_ref, held, sem) = rest[:-3], rest[-3:]
    n_dev, n_seg = rel_ref.shape
    n_own = table_ref.shape[0]
    me = me_ref[0]
    for c in range((n_dev - 1) * capacity):
        plan_ref[SEND, c] = 0
        plan_ref[TERM, c] = -1
        plan_ref[GIVEN, c] = -1
    spare = COLS - 1
    for s in range(n_dev):
        slots = [rel_ref[s, k] for k in range(n_seg)]
        owners = [lax.div(v, n_own) for v in slots]
        for k in range(n_seg):
            local = slots[k] - owners[k] * n_own
            order = jnp.int32(0)
            for q in range(k):
                order = order + (owners[q] == owners[k]).astype(jnp.int32)
            if s == 0:
                away = lax.rem(owners[k] - me + n_dev, n_dev)
                plan_ref[OWN, k] = jnp.where(away == 0, local, -1)
                from_owner = (n_dev - away - 1) * capacity + order
                plan_ref[SOURCE, k] = jnp.where(away == 0, local, n_own + from_owner)
                plan_ref[TERM, jnp.where(away == 0, spare, (away - 1) * capacity + order)] = k
            else:
                mine = owners[k] == me
                there = (n_dev - s - 1) * capacity + order
                plan_ref[SEND, jnp.where(mine, there, spare)] = local
                plan_ref[GIVEN, jnp.where(mine, (s - 1) * capacity + order, spare)] = local
    rows = [plan_ref[SEND, c] for c in range(len(outs) * capacity)]
    copy_rows(rows, table_ref, outs, held, sem)


def request(me, relative, table, capacity):
    count = relative.shape[0] - 1
    block = jax.ShapeDtypeStruct((capacity,) + table.shape[1:], table.dtype)
    *sends, plan = call(
        functools.partial(request_kernel, capacity),
        (me.reshape(1), relative, table),
        [SMEM, SMEM, ANYWHERE],
        out_shape=[block] * count + [jax.ShapeDtypeStruct((8, COLS), jnp.int32)],
        out_specs=[HBM] * count + [SMEM],
        scratch=copies_of(table, count * capacity),
        cost_estimate=cost(0, table.size * 4),
        name="request",
    )
    return sends, plan


def rows_kernel(row, plan_ref, table_ref, *rest):
    outs, (held, sem) = rest[:-2], rest[-2:]
    rows = [jnp.maximum(plan_ref[row, c], 0) for c in range(len(outs) * outs[0].shape[0])]
    copy_rows(rows, table_ref, outs, held, sem)


def rows_of(plan, row, table, count, capacity, after=()):
    block = jax.ShapeDtypeStruct((capacity,) + table.shape[1:], table.dtype)
    return call(
        functools.partial(rows_kernel, row),
        (plan, table),
        [SMEM, ANYWHERE],
        after,
        out_shape=[block] * count,
        out_specs=[HBM] * count,
        scratch=copies_of(table, count * capacity),
        cost_estimate=cost(0, table.size * 4),
        name="rows",
    )


def low_rank_kernel(plan_ref, act_ref, table_ref, *rest):
    blocks, (factor_ref, part_ref, sem) = rest[:-3], rest[-3:]
    n_own = table_ref.shape[0]
    n_seg, capacity = factor_ref.shape[0], blocks[0].shape[0]
    for k in range(n_seg):
        at = plan_ref[SOURCE, k]

        @pl.when(at < n_own)
        def _(k=k, at=at):
            pltpu.make_async_copy(table_ref.at[at], factor_ref.at[k], sem.at[k]).start()

        for n, ref in enumerate(blocks):
            slot = at - n_own - n * capacity

            @pl.when((slot >= 0) & (slot < capacity))
            def _(k=k, slot=slot, ref=ref):
                pltpu.make_async_copy(ref.at[slot], factor_ref.at[k], sem.at[k]).start()

    seg_rows = act_ref.shape[0] // n_seg
    for k in range(n_seg):
        pltpu.make_async_copy(table_ref.at[0], factor_ref.at[k], sem.at[k]).wait()
        part_ref[k] = lax.dot_general(
            factor_ref[k],
            act_ref[k * seg_rows : (k + 1) * seg_rows],
            (((1,), (1,)), ((), ())),
            preferred_element_type=F32,
        ).astype(part_ref.dtype)


def low_rank(plan, act, table, blocks, n_seg, after=()):
    _, rank, width = table.shape
    return call(
        low_rank_kernel,
        (plan, act, table, *blocks),
        [SMEM, VMEM] + [ANYWHERE] * (1 + len(blocks)),
        after,
        out_shape=[
            jax.ShapeDtypeStruct((n_seg, rank, width), BF16),
            jax.ShapeDtypeStruct((n_seg, rank, act.shape[0] // n_seg), BF16),
        ],
        out_specs=[VMEM, VMEM],
        scratch=[pltpu.SemaphoreType.DMA((n_seg,))],
        cost_estimate=cost(2 * act.size * rank, 4 * act.size),
        name="low_rank",
    )


def terms_kernel(live_ref, *rest):
    parts, (right_ref, act_ref, term_ref) = rest[:-3], rest[-3:]
    total = parts[0][0].astype(F32)
    for part in parts[1:]:
        total = total + part[0].astype(F32)
    column = lax.broadcasted_iota(jnp.int32, total.shape, 1)
    act = jnp.where(column < live_ref[pl.program_id(0)], total * SCALE, 0.0).astype(BF16)
    act_ref[0] = act
    term_ref[0] = jnp.dot(act, right_ref[...], preferred_element_type=F32).astype(BF16)


def make_terms(live_length, parts, right, after=()):
    n_seg, rank, seg_rows = parts[0].shape
    width = right.shape[1]
    small = pl.BlockSpec((1, rank, seg_rows), lambda k, *_: (k, 0, 0))
    return call(
        terms_kernel,
        (live_length, *parts, right),
        [small] * len(parts) + [pl.BlockSpec((seg_rows, width), lambda k, *_: (k, 0))],
        after,
        scalars=1,
        grid=(n_seg,),
        out_shape=[
            jax.ShapeDtypeStruct((n_seg, rank, seg_rows), BF16),
            jax.ShapeDtypeStruct((n_seg, rank, width), BF16),
        ],
        out_specs=[small, pl.BlockSpec((1, rank, width), lambda k, *_: (k, 0, 0))],
        cost_estimate=cost(2 * right.size * rank, 4 * right.size),
        name="terms",
    )


def total_kernel(plan_ref, terms_ref, *rest):
    blocks, out_ref = rest[:-1], rest[-1]
    capacity = blocks[0].shape[0]
    out_ref[...] = jnp.zeros_like(out_ref)
    sources = [(plan_ref[OWN, k], terms_ref, k) for k in range(terms_ref.shape[0])]
    for n, ref in enumerate(blocks):
        for j in range(capacity):
            sources.append((plan_ref[GIVEN, n * capacity + j], ref, j))
    for at, ref, k in sources:

        @pl.when(at >= 0)
        def _(at=at, ref=ref, k=k):
            out_ref[at] += ref[k].astype(F32)


def totals(plan, terms, blocks, n_own, after=()):
    n_seg, rank, width = terms.shape
    tile = min(512, width)

    def here(n):
        return pl.BlockSpec((n, rank, tile), lambda j: (0, 0, j))

    return call(
        total_kernel,
        (plan, terms, *blocks),
        [SMEM, here(n_seg)] + [here(b.shape[0]) for b in blocks],
        after,
        grid=(width // tile,),
        out_shape=jax.ShapeDtypeStruct((n_own, rank, width), F32),
        out_specs=here(n_own),
        cost_estimate=cost(0, 4 * terms.size),
        name="totals",
    )


def segment_sum(act_ref, factor_ref):
    return jnp.concatenate(
        [
            lax.dot_general(
                act_ref[k], factor_ref[k], (((0,), (0,)), ((), ())), preferred_element_type=F32
            )
            for k in range(act_ref.shape[0])
        ],
        axis=0,
    )


def forward_kernel(x_ref, w_ref, *rest):
    out = jnp.dot(x_ref[...], w_ref[...], preferred_element_type=F32)
    rest[-1][...] = out.astype(rest[-1].dtype)


def forward(x, weight, first, last, done=None, after=()):
    rows, width = x.shape
    full = weight.shape[1]
    args = [x, weight] + ([] if done is None else [done])
    return call(
        forward_kernel,
        args,
        [
            pl.BlockSpec((rows, width), lambda j: (0, 0)),
            pl.BlockSpec((width, TILE), lambda j: (0, first + j)),
        ]
        + [ANYWHERE] * (len(args) - 2),
        after,
        grid=(last - first,),
        out_shape=jax.ShapeDtypeStruct((rows, full), BF16),
        out_specs=pl.BlockSpec((rows, TILE), lambda j: (0, first + j)),
        input_output_aliases={} if done is None else {2: 0},
        cost_estimate=cost(2 * rows * width * (last - first) * TILE, 2 * width * full),
        name="forward",
    )


def backward_kernel(x_ref, w_ref, act_ref, factor_ref, out_ref):
    out = lax.dot_general(
        x_ref[...], w_ref[...], (((1,), (1,)), ((), ())), preferred_element_type=F32
    )
    out_ref[...] = (out + segment_sum(act_ref, factor_ref)).astype(out_ref.dtype)


def backward(x, weight, act, factors, after=()):
    rows, full = x.shape
    width = weight.shape[0]
    n_seg, rank, seg_rows = act.shape
    tile = min(256, width)
    return call(
        backward_kernel,
        (x, weight, act, factors),
        [
            pl.BlockSpec((rows, full), lambda j: (0, 0)),
            pl.BlockSpec((tile, full), lambda j: (j, 0)),
            pl.BlockSpec((n_seg, rank, seg_rows), lambda j: (0, 0, 0)),
            pl.BlockSpec((n_seg, rank, tile), lambda j: (0, 0, j)),
        ],
        after,
        grid=(width // tile,),
        out_shape=jax.ShapeDtypeStruct((rows, width), BF16),
        out_specs=pl.BlockSpec((rows, tile), lambda j: (0, j)),
        cost_estimate=cost(2 * rows * width * full, 2 * width * full),
        name="backward",
    )


def adapt_kernel(x_ref, act_ref, factor_ref, out_ref):
    out = x_ref[...].astype(F32) + segment_sum(act_ref, factor_ref)
    out_ref[...] = out.astype(out_ref.dtype)


def adapt(x, act, factors, after=()):
    rows, width = x.shape
    n_seg, rank, seg_rows = act.shape
    tile = min(512, width)
    here = pl.BlockSpec((rows, tile), lambda j: (0, j))
    return call(
        adapt_kernel,
        (x, act, factors),
        [
            here,
            pl.BlockSpec((n_seg, rank, seg_rows), lambda j: (0, 0, 0)),
            pl.BlockSpec((n_seg, rank, tile), lambda j: (0, 0, j)),
        ],
        after,
        grid=(width // tile,),
        out_shape=jax.ShapeDtypeStruct((rows, width), BF16),
        out_specs=here,
        cost_estimate=cost(2 * rows * width * rank, 4 * rows * width),
        name="adapt",
    )


def body(
    tokens,
    cotangent,
    weight,
    down_table,
    up_table,
    segment_adapter_id,
    segment_live_length,
    adapter_table_row,
):
    n_seg = segment_adapter_id.shape[0]
    n_own = down_table.shape[0]
    n_dev = lax.axis_size("dp")
    n_tensor = lax.axis_size("tensor")
    n_chips = n_tensor // 2
    capacity = max(2, n_seg // 2)

    def over_core(x):
        return lax.ppermute(x, "tensor", [(i, i ^ 1) for i in range(n_tensor)])

    def over_chips(x, s):
        pairs = [(i, (i // 2 + s) % n_chips * 2 + i % 2) for i in range(n_tensor)]
        return lax.ppermute(x, "tensor", pairs)

    def over_line(x, s):
        return lax.ppermute(x, "dp", [(i, (i + s) % n_dev) for i in range(n_dev)])

    shifts = range(1, n_dev)
    hops = range(1, n_chips)

    cot_rows = lax.all_gather(cotangent, "tensor", axis=1, tiled=True)

    one = segment_adapter_id[:, None] == jnp.arange(adapter_table_row.shape[0])[None, :]
    slots = jnp.sum(jnp.where(one, adapter_table_row[None, :], 0), axis=1).astype(jnp.int32)
    relative = jnp.stack([slots] + [over_line(slots, s) for s in shifts])

    down_t = jnp.swapaxes(down_table, 1, 2)
    me_dev = lax.axis_index("dp").astype(jnp.int32)
    sends, plan = request(me_dev, relative, down_t, capacity)
    down_got = [over_line(x, s) for x, s in zip(sends, shifts)]

    sends = rows_of(plan, SEND, up_table, n_dev - 1, capacity, [sends[-1]])
    up_got = [over_line(x, s) for x, s in zip(sends, shifts)]

    tiles = weight.shape[1] // TILE
    partial = forward(tokens, weight, 0, tiles - 1, after=[sends[-1]])
    partial = forward(tokens, weight, tiles - 1, tiles, partial, down_got)
    layer = lax.psum_scatter(partial, "tensor", scatter_dimension=1, tiled=True)

    def summed(part):
        part = (part.astype(F32) + over_core(part).astype(F32)).astype(BF16)
        return [part] + [over_chips(part, s) for s in hops]

    def give(terms):
        sends = rows_of(plan, TERM, terms, n_dev - 1, capacity)
        return sends, [over_line(x, s) for x, s in zip(sends, shifts)]

    down_seg, part = low_rank(plan, tokens, down_t, down_got, n_seg, [partial])
    act, up_terms = make_terms(segment_live_length, summed(part), cotangent)

    sends, up_back = give(up_terms)
    up_seg, part = low_rank(plan, cotangent, up_table, up_got, n_seg, [sends[-1]])
    grad, down_terms = make_terms(segment_live_length, summed(part), tokens)

    sends, down_back = give(down_terms)
    up_grad = totals(plan, up_terms, up_back, n_own, [sends[-1]])
    token_input_gradient = backward(cot_rows, weight, grad, down_seg, [up_grad])
    layer_result = adapt(layer, act, up_seg, [token_input_gradient])
    down_grad = totals(plan, down_terms, down_back, n_own, [layer_result])
    return layer_result, token_input_gradient, jnp.swapaxes(down_grad, 1, 2), up_grad


def solution(mesh):
    placed = (
        P(("groups", "dp"), "tensor"),
        P(("groups", "dp"), "tensor"),
        P("tensor", None),
        P(("groups", "dp"), "tensor", None),
        P(("groups", "dp"), None, "tensor"),
        P(("groups", "dp")),
        P(("groups", "dp")),
        P("groups"),
    )
    return jax.shard_map(
        body,
        mesh=mesh,
        in_specs=placed,
        out_specs=(
            P(("groups", "dp"), "tensor"),
            P(("groups", "dp"), "tensor"),
            P(("groups", "dp"), "tensor", None),
            P(("groups", "dp"), None, "tensor"),
        ),
        check_vma=False,
    )
```

```python
import functools

import jax
import jax.numpy as jnp
from jax import lax
from jax.experimental import pallas as pl
from jax.experimental.pallas import tpu as pltpu
from jax.sharding import PartitionSpec as P

SCALE = 0.015625
COLS = 128
TILE = 512
SEND, SOURCE, TERM, GIVEN, OWN = range(5)
F32, BF16 = jnp.float32, jnp.bfloat16
SMEM = pl.BlockSpec(memory_space=pltpu.SMEM)
VMEM = pl.BlockSpec(memory_space=pltpu.VMEM)
ANYWHERE = pl.BlockSpec(memory_space=pl.ANY)
HBM = pl.BlockSpec(memory_space=pltpu.HBM)
PARAMS = pltpu.CompilerParams(vmem_limit_bytes=56 << 20)


def cost(flops, nbytes):
    return pl.CostEstimate(flops=flops, bytes_accessed=nbytes, transcendentals=0)


def call(kernel, args, in_specs, after=(), scalars=0, grid=(), out_specs=None, scratch=(), **rest):
    n_in = len(args)

    def body(*refs):
        kernel(*refs[:n_in], *refs[n_in + len(after) :])

    return pl.pallas_call(
        body,
        grid_spec=pltpu.PrefetchScalarGridSpec(
            num_scalar_prefetch=scalars,
            grid=grid,
            in_specs=list(in_specs) + [ANYWHERE] * len(after),
            out_specs=out_specs,
            scratch_shapes=list(scratch),
        ),
        compiler_params=PARAMS,
        **rest,
    )(*args, *after)


def copy_rows(rows, table_ref, outs, held, sem):
    capacity = outs[0].shape[0]
    reads = [
        pltpu.make_async_copy(table_ref.at[row], held.at[c], sem.at[0, c])
        for c, row in enumerate(rows)
    ]
    writes = [
        pltpu.make_async_copy(held.at[c], outs[c // capacity].at[c % capacity], sem.at[1, c])
        for c in range(len(rows))
    ]
    for read in reads:
        read.start()

    def finish_copies():
        for read, write in zip(reads, writes):
            read.wait()
            write.start()
        for write in writes:
            write.wait()

    return finish_copies


def copies_of(table, count):
    return [
        pltpu.VMEM((count,) + table.shape[1:], table.dtype),
        pltpu.SemaphoreType.DMA((2, count)),
    ]


def request_kernel(capacity, me_ref, rel_ref, table_ref, *rest):
    outs, (plan_ref, held, sem) = rest[:-3], rest[-3:]
    n_dev, n_seg = rel_ref.shape
    n_own = table_ref.shape[0]
    me = me_ref[0]
    spare = COLS - 1
    for c in range((n_dev - 1) * capacity):
        for row in (SEND, TERM, GIVEN):
            plan_ref[row, c] = 0 if row == SEND else -1
    for s in range(1, n_dev):
        slots = [rel_ref[s, k] for k in range(n_seg)]
        order = jnp.int32(0)
        for slot in slots:
            mine = lax.div(slot, n_own) == me
            local = slot - me * n_own
            there = (n_dev - s - 1) * capacity + order
            plan_ref[SEND, jnp.where(mine, there, spare)] = local
            plan_ref[GIVEN, jnp.where(mine, (s - 1) * capacity + order, spare)] = local
            order = order + mine.astype(jnp.int32)
    rows = [plan_ref[SEND, c] for c in range(len(outs) * capacity)]
    finish_copies = copy_rows(rows, table_ref, outs, held, sem)
    slots = [rel_ref[0, k] for k in range(n_seg)]
    owners = [lax.div(v, n_own) for v in slots]
    for k in range(n_seg):
        local = slots[k] - owners[k] * n_own
        order = jnp.int32(0)
        for q in range(k):
            order = order + (owners[q] == owners[k]).astype(jnp.int32)
        away = lax.rem(owners[k] - me + n_dev, n_dev)
        plan_ref[OWN, k] = jnp.where(away == 0, local, -1)
        from_owner = (n_dev - away - 1) * capacity + order
        plan_ref[SOURCE, k] = jnp.where(away == 0, local, n_own + from_owner)
        plan_ref[TERM, jnp.where(away == 0, spare, (away - 1) * capacity + order)] = k
    finish_copies()


def request(me, relative, table, capacity):
    count = relative.shape[0] - 1
    block = jax.ShapeDtypeStruct((capacity,) + table.shape[1:], table.dtype)
    *sends, plan = call(
        functools.partial(request_kernel, capacity),
        (me.reshape(1), relative, table),
        [SMEM, SMEM, ANYWHERE],
        out_shape=[block] * count + [jax.ShapeDtypeStruct((8, COLS), jnp.int32)],
        out_specs=[HBM] * count + [SMEM],
        scratch=copies_of(table, count * capacity),
        cost_estimate=cost(0, table.size * 4),
        name="request",
    )
    return sends, plan


def rows_kernel(row, plan_ref, table_ref, *rest):
    outs, (held, sem) = rest[:-2], rest[-2:]
    rows = [jnp.maximum(plan_ref[row, c], 0) for c in range(len(outs) * outs[0].shape[0])]
    copy_rows(rows, table_ref, outs, held, sem)()


def rows_of(plan, row, table, count, capacity, after=()):
    block = jax.ShapeDtypeStruct((capacity,) + table.shape[1:], table.dtype)
    return call(
        functools.partial(rows_kernel, row),
        (plan, table),
        [SMEM, ANYWHERE],
        after,
        out_shape=[block] * count,
        out_specs=[HBM] * count,
        scratch=copies_of(table, count * capacity),
        cost_estimate=cost(0, table.size * 4),
        name="rows",
    )


def low_rank_kernel(plan_ref, act_ref, table_ref, *rest):
    blocks, (factor_ref, part_ref, sem) = rest[:-3], rest[-3:]
    n_own = table_ref.shape[0]
    n_seg, capacity = factor_ref.shape[0], blocks[0].shape[0]
    for k in range(n_seg):
        at = plan_ref[SOURCE, k]

        @pl.when(at < n_own)
        def _(k=k, at=at):
            pltpu.make_async_copy(table_ref.at[at], factor_ref.at[k], sem.at[k]).start()

        for n, ref in enumerate(blocks):
            slot = at - n_own - n * capacity

            @pl.when((slot >= 0) & (slot < capacity))
            def _(k=k, slot=slot, ref=ref):
                pltpu.make_async_copy(ref.at[slot], factor_ref.at[k], sem.at[k]).start()

    seg_rows = act_ref.shape[0] // n_seg
    for k in range(n_seg):
        pltpu.make_async_copy(table_ref.at[0], factor_ref.at[k], sem.at[k]).wait()
        part_ref[k] = lax.dot_general(
            factor_ref[k],
            act_ref[k * seg_rows : (k + 1) * seg_rows],
            (((1,), (1,)), ((), ())),
            preferred_element_type=F32,
        ).astype(part_ref.dtype)


def low_rank(plan, act, table, blocks, n_seg, after=()):
    _, rank, width = table.shape
    return call(
        low_rank_kernel,
        (plan, act, table, *blocks),
        [SMEM, VMEM] + [ANYWHERE] * (1 + len(blocks)),
        after,
        out_shape=[
            jax.ShapeDtypeStruct((n_seg, rank, width), BF16),
            jax.ShapeDtypeStruct((n_seg, rank, act.shape[0] // n_seg), BF16),
        ],
        out_specs=[VMEM, VMEM],
        scratch=[pltpu.SemaphoreType.DMA((n_seg,))],
        cost_estimate=cost(2 * act.size * rank, 4 * act.size),
        name="low_rank",
    )


def terms_kernel(live_ref, *rest):
    parts, (right_ref, act_ref, term_ref) = rest[:-3], rest[-3:]
    total = parts[0][0].astype(F32)
    for part in parts[1:]:
        total = total + part[0].astype(F32)
    column = lax.broadcasted_iota(jnp.int32, total.shape, 1)
    act = jnp.where(column < live_ref[pl.program_id(0)], total * SCALE, 0.0).astype(BF16)
    act_ref[0] = act
    term_ref[0] = jnp.dot(act, right_ref[...], preferred_element_type=F32).astype(BF16)


def make_terms(live_length, parts, right, after=()):
    n_seg, rank, seg_rows = parts[0].shape
    width = right.shape[1]
    small = pl.BlockSpec((1, rank, seg_rows), lambda k, *_: (k, 0, 0))
    return call(
        terms_kernel,
        (live_length, *parts, right),
        [small] * len(parts) + [pl.BlockSpec((seg_rows, width), lambda k, *_: (k, 0))],
        after,
        scalars=1,
        grid=(n_seg,),
        out_shape=[
            jax.ShapeDtypeStruct((n_seg, rank, seg_rows), BF16),
            jax.ShapeDtypeStruct((n_seg, rank, width), BF16),
        ],
        out_specs=[small, pl.BlockSpec((1, rank, width), lambda k, *_: (k, 0, 0))],
        cost_estimate=cost(2 * right.size * rank, 4 * right.size),
        name="terms",
    )


def total_kernel(plan_ref, terms_ref, *rest):
    blocks, out_ref = rest[:-1], rest[-1]
    capacity = blocks[0].shape[0]
    out_ref[...] = jnp.zeros_like(out_ref)
    sources = [(plan_ref[OWN, k], terms_ref, k) for k in range(terms_ref.shape[0])]
    for n, ref in enumerate(blocks):
        for j in range(capacity):
            sources.append((plan_ref[GIVEN, n * capacity + j], ref, j))
    for at, ref, k in sources:

        @pl.when(at >= 0)
        def _(at=at, ref=ref, k=k):
            out_ref[at] += ref[k].astype(F32)


def totals(plan, terms, blocks, n_own, after=()):
    n_seg, rank, width = terms.shape
    tile = min(512, width)

    def here(n):
        return pl.BlockSpec((n, rank, tile), lambda j: (0, 0, j))

    return call(
        total_kernel,
        (plan, terms, *blocks),
        [SMEM, here(n_seg)] + [here(b.shape[0]) for b in blocks],
        after,
        grid=(width // tile,),
        out_shape=jax.ShapeDtypeStruct((n_own, rank, width), F32),
        out_specs=here(n_own),
        cost_estimate=cost(0, 4 * terms.size),
        name="totals",
    )


def segment_sum(act_ref, factor_ref):
    return jnp.concatenate(
        [
            lax.dot_general(
                act_ref[k], factor_ref[k], (((0,), (0,)), ((), ())), preferred_element_type=F32
            )
            for k in range(act_ref.shape[0])
        ],
        axis=0,
    )


def forward_kernel(x_ref, w_ref, out_ref):
    out_ref[...] = jnp.dot(x_ref[...], w_ref[...], preferred_element_type=F32).astype(out_ref.dtype)


def forward(x, weight, after=()):
    rows, width = x.shape
    full = weight.shape[1]
    return call(
        forward_kernel,
        (x, weight),
        [
            pl.BlockSpec((rows, width), lambda j: (0, 0)),
            pl.BlockSpec((width, TILE), lambda j: (0, j)),
        ],
        after,
        grid=(full // TILE,),
        out_shape=jax.ShapeDtypeStruct((rows, full), BF16),
        out_specs=pl.BlockSpec((rows, TILE), lambda j: (0, j)),
        cost_estimate=cost(2 * rows * width * full, 2 * width * full),
        name="forward",
    )


def held_back(x, after):
    return call(
        lambda x_ref, out_ref: None,
        (x,),
        [ANYWHERE],
        after,
        out_shape=jax.ShapeDtypeStruct(x.shape, x.dtype),
        out_specs=ANYWHERE,
        input_output_aliases={0: 0},
        cost_estimate=cost(0, 0),
        name="held_back",
    )


def backward_kernel(x_ref, w_ref, act_ref, factor_ref, out_ref):
    out = lax.dot_general(
        x_ref[...], w_ref[...], (((1,), (1,)), ((), ())), preferred_element_type=F32
    )
    out_ref[...] = (out + segment_sum(act_ref, factor_ref)).astype(out_ref.dtype)


def backward(x, weight, act, factors, after=()):
    rows, full = x.shape
    width = weight.shape[0]
    n_seg, rank, seg_rows = act.shape
    tile = min(256, width)
    return call(
        backward_kernel,
        (x, weight, act, factors),
        [
            pl.BlockSpec((rows, full), lambda j: (0, 0)),
            pl.BlockSpec((tile, full), lambda j: (j, 0)),
            pl.BlockSpec((n_seg, rank, seg_rows), lambda j: (0, 0, 0)),
            pl.BlockSpec((n_seg, rank, tile), lambda j: (0, 0, j)),
        ],
        after,
        grid=(width // tile,),
        out_shape=jax.ShapeDtypeStruct((rows, width), BF16),
        out_specs=pl.BlockSpec((rows, tile), lambda j: (0, j)),
        cost_estimate=cost(2 * rows * width * full, 2 * width * full),
        name="backward",
    )


def adapt_kernel(x_ref, act_ref, factor_ref, out_ref):
    out = x_ref[...].astype(F32) + segment_sum(act_ref, factor_ref)
    out_ref[...] = out.astype(out_ref.dtype)


def adapt(x, act, factors, after=()):
    rows, width = x.shape
    n_seg, rank, seg_rows = act.shape
    tile = min(512, width)
    here = pl.BlockSpec((rows, tile), lambda j: (0, j))
    return call(
        adapt_kernel,
        (x, act, factors),
        [
            here,
            pl.BlockSpec((n_seg, rank, seg_rows), lambda j: (0, 0, 0)),
            pl.BlockSpec((n_seg, rank, tile), lambda j: (0, 0, j)),
        ],
        after,
        grid=(width // tile,),
        out_shape=jax.ShapeDtypeStruct((rows, width), BF16),
        out_specs=here,
        cost_estimate=cost(2 * rows * width * rank, 4 * rows * width),
        name="adapt",
    )


def body(
    tokens,
    cotangent,
    weight,
    down_table,
    up_table,
    segment_adapter_id,
    segment_live_length,
    adapter_table_row,
):
    n_seg = segment_adapter_id.shape[0]
    n_own = down_table.shape[0]
    n_dev = lax.axis_size("dp")
    n_tensor = lax.axis_size("tensor")
    n_chips = n_tensor // 2
    capacity = max(2, n_seg // 2)

    def over_core(x):
        return lax.ppermute(x, "tensor", [(i, i ^ 1) for i in range(n_tensor)])

    def over_chips(x, s):
        pairs = [(i, (i // 2 + s) % n_chips * 2 + i % 2) for i in range(n_tensor)]
        return lax.ppermute(x, "tensor", pairs)

    def over_line(x, s):
        return lax.ppermute(x, "dp", [(i, (i + s) % n_dev) for i in range(n_dev)])

    shifts = range(1, n_dev)
    hops = range(1, n_chips)

    cot_rows = lax.all_gather(cotangent, "tensor", axis=1, tiled=True)

    one = segment_adapter_id[:, None] == jnp.arange(adapter_table_row.shape[0])[None, :]
    slots = jnp.sum(jnp.where(one, adapter_table_row[None, :], 0), axis=1).astype(jnp.int32)
    relative = jnp.stack([slots] + [over_line(slots, s) for s in shifts])

    down_t = jnp.swapaxes(down_table, 1, 2)
    me_dev = lax.axis_index("dp").astype(jnp.int32)
    sends, plan = request(me_dev, relative, down_t, capacity)
    down_got = [over_line(x, s) for x, s in zip(sends, shifts)]

    sends = rows_of(plan, SEND, up_table, n_dev - 1, capacity, [sends[-1]])
    up_got = [over_line(x, s) for x, s in zip(sends, shifts)]

    partial = held_back(forward(tokens, weight, [sends[-1]]), down_got)
    layer = lax.psum_scatter(partial, "tensor", scatter_dimension=1, tiled=True)

    def summed(part):
        part = (part.astype(F32) + over_core(part).astype(F32)).astype(BF16)
        return [part] + [over_chips(part, s) for s in hops]

    def give(terms):
        sends = rows_of(plan, TERM, terms, n_dev - 1, capacity)
        return sends, [over_line(x, s) for x, s in zip(sends, shifts)]

    down_seg, part = low_rank(plan, tokens, down_t, down_got, n_seg, [partial])
    act, up_terms = make_terms(segment_live_length, summed(part), cotangent)

    sends, up_back = give(up_terms)
    up_seg, part = low_rank(plan, cotangent, up_table, up_got, n_seg, [sends[-1]])
    grad, down_terms = make_terms(segment_live_length, summed(part), tokens)

    sends, down_back = give(down_terms)
    up_grad = totals(plan, up_terms, up_back, n_own, [sends[-1]])
    token_input_gradient = backward(cot_rows, weight, grad, down_seg, [up_grad])
    layer_result = adapt(layer, act, up_seg, [token_input_gradient])
    down_grad = totals(plan, down_terms, down_back, n_own, [layer_result])
    return layer_result, token_input_gradient, jnp.swapaxes(down_grad, 1, 2), up_grad


def solution(mesh):
    placed = (
        P(("groups", "dp"), "tensor"),
        P(("groups", "dp"), "tensor"),
        P("tensor", None),
        P(("groups", "dp"), "tensor", None),
        P(("groups", "dp"), None, "tensor"),
        P(("groups", "dp")),
        P(("groups", "dp")),
        P("groups"),
    )
    return jax.shard_map(
        body,
        mesh=mesh,
        in_specs=placed,
        out_specs=(
            P(("groups", "dp"), "tensor"),
            P(("groups", "dp"), "tensor"),
            P(("groups", "dp"), "tensor", None),
            P(("groups", "dp"), None, "tensor"),
        ),
        check_vma=False,
    )
```

```python
import functools

import jax
import jax.numpy as jnp
from jax import lax
from jax.experimental import pallas as pl
from jax.experimental.pallas import tpu as pltpu
from jax.sharding import PartitionSpec as P

SCALE = 0.015625
COLS = 128
TILE = 512
SEND, SOURCE, TERM, GIVEN, OWN = range(5)
F32, BF16 = jnp.float32, jnp.bfloat16
SMEM = pl.BlockSpec(memory_space=pltpu.SMEM)
VMEM = pl.BlockSpec(memory_space=pltpu.VMEM)
ANYWHERE = pl.BlockSpec(memory_space=pl.ANY)
HBM = pl.BlockSpec(memory_space=pltpu.HBM)
PARAMS = pltpu.CompilerParams(vmem_limit_bytes=56 << 20)


def cost(flops, nbytes):
    return pl.CostEstimate(flops=flops, bytes_accessed=nbytes, transcendentals=0)


def call(kernel, args, in_specs, after=(), scalars=0, grid=(), out_specs=None, scratch=(), **rest):
    n_in = len(args)

    def body(*refs):
        kernel(*refs[:n_in], *refs[n_in + len(after) :])

    return pl.pallas_call(
        body,
        grid_spec=pltpu.PrefetchScalarGridSpec(
            num_scalar_prefetch=scalars,
            grid=grid,
            in_specs=list(in_specs) + [ANYWHERE] * len(after),
            out_specs=out_specs,
            scratch_shapes=list(scratch),
        ),
        compiler_params=PARAMS,
        **rest,
    )(*args, *after)


def copy_rows(rows, table_ref, outs, held, sem):
    capacity = outs[0].shape[0]
    reads = [
        pltpu.make_async_copy(table_ref.at[row], held.at[c], sem.at[0, c])
        for c, row in enumerate(rows)
    ]
    writes = [
        pltpu.make_async_copy(held.at[c], outs[c // capacity].at[c % capacity], sem.at[1, c])
        for c in range(len(rows))
    ]
    for read in reads:
        read.start()

    def finish_copies():
        for read, write in zip(reads, writes):
            read.wait()
            write.start()
        for write in writes:
            write.wait()

    return finish_copies


def copies_of(table, count):
    return [
        pltpu.VMEM((count,) + table.shape[1:], table.dtype),
        pltpu.SemaphoreType.DMA((2, count)),
    ]


def request_kernel(capacity, n_dev, me_ref, row_ref, *rest):
    id_refs, table_ref = rest[:n_dev], rest[n_dev]
    outs, (plan_ref, held, sem) = rest[n_dev + 1 : -3], rest[-3:]
    n_seg = id_refs[0].shape[0]
    n_own = table_ref.shape[0]
    me = me_ref[0]
    spare = COLS - 1
    for c in range((n_dev - 1) * capacity):
        for row in (SEND, TERM, GIVEN):
            plan_ref[row, c] = 0 if row == SEND else -1
    for s in range(1, n_dev):
        slots = [row_ref[id_refs[s][k]] for k in range(n_seg)]
        order = jnp.int32(0)
        for slot in slots:
            mine = lax.div(slot, n_own) == me
            local = slot - me * n_own
            there = (n_dev - s - 1) * capacity + order
            plan_ref[SEND, jnp.where(mine, there, spare)] = local
            plan_ref[GIVEN, jnp.where(mine, (s - 1) * capacity + order, spare)] = local
            order = order + mine.astype(jnp.int32)
    rows = [plan_ref[SEND, c] for c in range(len(outs) * capacity)]
    finish_copies = copy_rows(rows, table_ref, outs, held, sem)
    slots = [row_ref[id_refs[0][k]] for k in range(n_seg)]
    owners = [lax.div(v, n_own) for v in slots]
    for k in range(n_seg):
        local = slots[k] - owners[k] * n_own
        order = jnp.int32(0)
        for q in range(k):
            order = order + (owners[q] == owners[k]).astype(jnp.int32)
        away = lax.rem(owners[k] - me + n_dev, n_dev)
        plan_ref[OWN, k] = jnp.where(away == 0, local, -1)
        from_owner = (n_dev - away - 1) * capacity + order
        plan_ref[SOURCE, k] = jnp.where(away == 0, local, n_own + from_owner)
        plan_ref[TERM, jnp.where(away == 0, spare, (away - 1) * capacity + order)] = k
    finish_copies()


def request(me, table_row, ids, table, capacity):
    n_dev = len(ids)
    count = n_dev - 1
    block = jax.ShapeDtypeStruct((capacity,) + table.shape[1:], table.dtype)
    *sends, plan = call(
        functools.partial(request_kernel, capacity, n_dev),
        (me.reshape(1), table_row, *ids, table),
        [SMEM] * (2 + n_dev) + [ANYWHERE],
        out_shape=[block] * count + [jax.ShapeDtypeStruct((8, COLS), jnp.int32)],
        out_specs=[HBM] * count + [SMEM],
        scratch=copies_of(table, count * capacity),
        cost_estimate=cost(0, table.size * 4),
        name="request",
    )
    return sends, plan


def rows_kernel(row, plan_ref, table_ref, *rest):
    outs, (held, sem) = rest[:-2], rest[-2:]
    rows = [jnp.maximum(plan_ref[row, c], 0) for c in range(len(outs) * outs[0].shape[0])]
    copy_rows(rows, table_ref, outs, held, sem)()


def rows_of(plan, row, table, count, capacity, after=()):
    block = jax.ShapeDtypeStruct((capacity,) + table.shape[1:], table.dtype)
    return call(
        functools.partial(rows_kernel, row),
        (plan, table),
        [SMEM, ANYWHERE],
        after,
        out_shape=[block] * count,
        out_specs=[HBM] * count,
        scratch=copies_of(table, count * capacity),
        cost_estimate=cost(0, table.size * 4),
        name="rows",
    )


def low_rank_kernel(plan_ref, act_ref, table_ref, *rest):
    blocks, (factor_ref, part_ref, sem) = rest[:-3], rest[-3:]
    n_own = table_ref.shape[0]
    n_seg, capacity = factor_ref.shape[0], blocks[0].shape[0]
    for k in range(n_seg):
        at = plan_ref[SOURCE, k]

        @pl.when(at < n_own)
        def _(k=k, at=at):
            pltpu.make_async_copy(table_ref.at[at], factor_ref.at[k], sem.at[k]).start()

        for n, ref in enumerate(blocks):
            slot = at - n_own - n * capacity

            @pl.when((slot >= 0) & (slot < capacity))
            def _(k=k, slot=slot, ref=ref):
                pltpu.make_async_copy(ref.at[slot], factor_ref.at[k], sem.at[k]).start()

    seg_rows = act_ref.shape[0] // n_seg
    for k in range(n_seg):
        pltpu.make_async_copy(table_ref.at[0], factor_ref.at[k], sem.at[k]).wait()
        part_ref[k] = lax.dot_general(
            factor_ref[k],
            act_ref[k * seg_rows : (k + 1) * seg_rows],
            (((1,), (1,)), ((), ())),
            preferred_element_type=F32,
        ).astype(part_ref.dtype)


def low_rank(plan, act, table, blocks, n_seg, after=()):
    _, rank, width = table.shape
    return call(
        low_rank_kernel,
        (plan, act, table, *blocks),
        [SMEM, VMEM] + [ANYWHERE] * (1 + len(blocks)),
        after,
        out_shape=[
            jax.ShapeDtypeStruct((n_seg, rank, width), BF16),
            jax.ShapeDtypeStruct((n_seg, rank, act.shape[0] // n_seg), BF16),
        ],
        out_specs=[VMEM, VMEM],
        scratch=[pltpu.SemaphoreType.DMA((n_seg,))],
        cost_estimate=cost(2 * act.size * rank, 4 * act.size),
        name="low_rank",
    )


def terms_kernel(live_ref, *rest):
    parts, (right_ref, act_ref, term_ref) = rest[:-3], rest[-3:]
    total = parts[0][0].astype(F32)
    for part in parts[1:]:
        total = total + part[0].astype(F32)
    column = lax.broadcasted_iota(jnp.int32, total.shape, 1)
    act = jnp.where(column < live_ref[pl.program_id(0)], total * SCALE, 0.0).astype(BF16)
    act_ref[0] = act
    term_ref[0] = jnp.dot(act, right_ref[...], preferred_element_type=F32).astype(BF16)


def make_terms(live_length, parts, right, after=()):
    n_seg, rank, seg_rows = parts[0].shape
    width = right.shape[1]
    small = pl.BlockSpec((1, rank, seg_rows), lambda k, *_: (k, 0, 0))
    return call(
        terms_kernel,
        (live_length, *parts, right),
        [small] * len(parts) + [pl.BlockSpec((seg_rows, width), lambda k, *_: (k, 0))],
        after,
        scalars=1,
        grid=(n_seg,),
        out_shape=[
            jax.ShapeDtypeStruct((n_seg, rank, seg_rows), BF16),
            jax.ShapeDtypeStruct((n_seg, rank, width), BF16),
        ],
        out_specs=[small, pl.BlockSpec((1, rank, width), lambda k, *_: (k, 0, 0))],
        cost_estimate=cost(2 * right.size * rank, 4 * right.size),
        name="terms",
    )


def total_kernel(plan_ref, terms_ref, *rest):
    blocks, out_ref = rest[:-1], rest[-1]
    capacity = blocks[0].shape[0]
    mine = pl.program_id(0)
    out_ref[...] = jnp.zeros_like(out_ref)
    sources = [(plan_ref[OWN, k], terms_ref, k) for k in range(terms_ref.shape[0])]
    for n, ref in enumerate(blocks):
        for j in range(capacity):
            sources.append((plan_ref[GIVEN, (n - 1) % len(blocks) * capacity + j], ref, j))
    for at, ref, k in sources:

        @pl.when(at == mine)
        def _(ref=ref, k=k):
            out_ref[0] += ref[k].astype(F32)


def totals(plan, terms, blocks, n_own, after=()):
    blocks = rotated(blocks)
    _, rank, width = terms.shape
    return call(
        total_kernel,
        (plan, terms, *blocks),
        [SMEM] + [VMEM] * (1 + len(blocks)),
        after,
        grid=(n_own,),
        out_shape=jax.ShapeDtypeStruct((n_own, rank, width), F32),
        out_specs=pl.BlockSpec((1, rank, width), lambda j: (j, 0, 0)),
        cost_estimate=cost(0, 4 * terms.size),
        name="totals",
    )


def segment_sum(act_ref, factor_ref):
    return jnp.concatenate(
        [
            lax.dot_general(
                act_ref[k], factor_ref[k], (((0,), (0,)), ((), ())), preferred_element_type=F32
            )
            for k in range(act_ref.shape[0])
        ],
        axis=0,
    )


def forward_kernel(x_ref, w_ref, out_ref):
    out_ref[...] = jnp.dot(x_ref[...], w_ref[...], preferred_element_type=F32).astype(out_ref.dtype)


def forward(x, weight, after=()):
    rows, width = x.shape
    full = weight.shape[1]
    return call(
        forward_kernel,
        (x, weight),
        [
            pl.BlockSpec((rows, width), lambda j: (0, 0)),
            pl.BlockSpec((width, TILE), lambda j: (0, j)),
        ],
        after,
        grid=(full // TILE,),
        out_shape=jax.ShapeDtypeStruct((rows, full), BF16),
        out_specs=pl.BlockSpec((rows, TILE), lambda j: (0, j)),
        cost_estimate=cost(2 * rows * width * full, 2 * width * full),
        name="forward",
    )


def rotated(blocks):
    return [blocks[-1], *blocks[:-1]]


def held_back(arrays, after):
    n = len(arrays)
    return call(
        lambda *refs: None,
        arrays,
        [ANYWHERE] * n,
        after,
        out_shape=[jax.ShapeDtypeStruct(x.shape, x.dtype) for x in arrays],
        out_specs=[ANYWHERE] * n,
        input_output_aliases={i: i for i in range(n)},
        cost_estimate=cost(0, 0),
        name="held_back",
    )


def backward_kernel(x_ref, w_ref, act_ref, factor_ref, out_ref):
    out = lax.dot_general(
        x_ref[...], w_ref[...], (((1,), (1,)), ((), ())), preferred_element_type=F32
    )
    out_ref[...] = (out + segment_sum(act_ref, factor_ref)).astype(out_ref.dtype)


def backward(x, weight, act, factors, after=()):
    rows, full = x.shape
    width = weight.shape[0]
    n_seg, rank, seg_rows = act.shape
    tile = min(256, width)
    return call(
        backward_kernel,
        (x, weight, act, factors),
        [
            pl.BlockSpec((rows, full), lambda j: (0, 0)),
            pl.BlockSpec((tile, full), lambda j: (j, 0)),
            pl.BlockSpec((n_seg, rank, seg_rows), lambda j: (0, 0, 0)),
            pl.BlockSpec((n_seg, rank, tile), lambda j: (0, 0, j)),
        ],
        after,
        grid=(width // tile,),
        out_shape=jax.ShapeDtypeStruct((rows, width), BF16),
        out_specs=pl.BlockSpec((rows, tile), lambda j: (0, j)),
        cost_estimate=cost(2 * rows * width * full, 2 * width * full),
        name="backward",
    )


def adapt_kernel(x_ref, act_ref, factor_ref, out_ref):
    out = x_ref[...].astype(F32) + segment_sum(act_ref, factor_ref)
    out_ref[...] = out.astype(out_ref.dtype)


def adapt(x, act, factors, after=()):
    rows, width = x.shape
    n_seg, rank, seg_rows = act.shape
    tile = min(512, width)
    here = pl.BlockSpec((rows, tile), lambda j: (0, j))
    return call(
        adapt_kernel,
        (x, act, factors),
        [
            here,
            pl.BlockSpec((n_seg, rank, seg_rows), lambda j: (0, 0, 0)),
            pl.BlockSpec((n_seg, rank, tile), lambda j: (0, 0, j)),
        ],
        after,
        grid=(width // tile,),
        out_shape=jax.ShapeDtypeStruct((rows, width), BF16),
        out_specs=here,
        cost_estimate=cost(2 * rows * width * rank, 4 * rows * width),
        name="adapt",
    )


def body(
    tokens,
    cotangent,
    weight,
    down_table,
    up_table,
    segment_adapter_id,
    segment_live_length,
    adapter_table_row,
):
    n_seg = segment_adapter_id.shape[0]
    n_own = down_table.shape[0]
    n_dev = lax.axis_size("dp")
    n_tensor = lax.axis_size("tensor")
    n_chips = n_tensor // 2
    capacity = max(2, n_seg // 2)

    def over_core(x):
        return lax.ppermute(x, "tensor", [(i, i ^ 1) for i in range(n_tensor)])

    def over_chips(x, s):
        pairs = [(i, (i // 2 + s) % n_chips * 2 + i % 2) for i in range(n_tensor)]
        return lax.ppermute(x, "tensor", pairs)

    def over_line(x, s):
        return lax.ppermute(x, "dp", [(i, (i + s) % n_dev) for i in range(n_dev)])

    shifts = range(1, n_dev)
    hops = range(1, n_chips)

    cot_rows = lax.all_gather(cotangent, "tensor", axis=1, tiled=True)

    ids = [segment_adapter_id] + [over_line(segment_adapter_id, s) for s in shifts]

    down_t = jnp.swapaxes(down_table, 1, 2)
    me_dev = lax.axis_index("dp").astype(jnp.int32)
    sends, plan = request(me_dev, adapter_table_row, ids, down_t, capacity)
    down_got = [over_line(x, s) for x, s in zip(sends, shifts)]

    sends = rows_of(plan, SEND, up_table, n_dev - 1, capacity, [sends[-1]])
    up_got = [over_line(x, s) for x, s in zip(sends, shifts)]

    (partial,) = held_back([forward(tokens, weight, [sends[-1]])], rotated(down_got))
    layer = lax.psum_scatter(partial, "tensor", scatter_dimension=1, tiled=True)

    def summed(part):
        part = (part.astype(F32) + over_core(part).astype(F32)).astype(BF16)
        return [part] + [over_chips(part, s) for s in hops]

    def give(terms, after):
        sends = held_back(rows_of(plan, TERM, terms, n_dev - 1, capacity), rotated(after))
        return sends, [over_line(x, s) for x, s in zip(sends, shifts)]

    down_seg, part = low_rank(plan, tokens, down_t, down_got, n_seg, [partial])
    act, up_terms = make_terms(segment_live_length, summed(part), cotangent)

    sends, up_back = give(up_terms, up_got)
    up_seg, part = low_rank(plan, cotangent, up_table, up_got, n_seg, [sends[-1]])
    grad, down_terms = make_terms(segment_live_length, summed(part), tokens)

    sends, down_back = give(down_terms, up_back)
    up_grad = totals(plan, up_terms, up_back, n_own, [sends[-1]])
    token_input_gradient = backward(cot_rows, weight, grad, down_seg, [up_grad])
    layer_result = adapt(layer, act, up_seg, [token_input_gradient])
    down_grad = totals(plan, down_terms, down_back, n_own, [layer_result])
    return layer_result, token_input_gradient, jnp.swapaxes(down_grad, 1, 2), up_grad


def solution(mesh):
    placed = (
        P(("groups", "dp"), "tensor"),
        P(("groups", "dp"), "tensor"),
        P("tensor", None),
        P(("groups", "dp"), "tensor", None),
        P(("groups", "dp"), None, "tensor"),
        P(("groups", "dp")),
        P(("groups", "dp")),
        P("groups"),
    )
    return jax.shard_map(
        body,
        mesh=mesh,
        in_specs=placed,
        out_specs=(
            P(("groups", "dp"), "tensor"),
            P(("groups", "dp"), "tensor"),
            P(("groups", "dp"), "tensor", None),
            P(("groups", "dp"), None, "tensor"),
        ),
        check_vma=False,
    )
```

```python
import functools

import jax
import jax.numpy as jnp
from jax import lax
from jax.experimental import pallas as pl
from jax.experimental.pallas import tpu as pltpu
from jax.sharding import PartitionSpec as P

SCALE = 0.015625
COLS = 128
TILE = 512
SEND, SOURCE, TERM, GIVEN, OWN = range(5)
F32, BF16 = jnp.float32, jnp.bfloat16
SMEM = pl.BlockSpec(memory_space=pltpu.SMEM)
VMEM = pl.BlockSpec(memory_space=pltpu.VMEM)
ANYWHERE = pl.BlockSpec(memory_space=pl.ANY)
HBM = pl.BlockSpec(memory_space=pltpu.HBM)
PARAMS = pltpu.CompilerParams(vmem_limit_bytes=56 << 20)


def cost(flops, nbytes):
    return pl.CostEstimate(flops=flops, bytes_accessed=nbytes, transcendentals=0)


def call(kernel, args, in_specs, after=(), scalars=0, grid=(), out_specs=None, scratch=(), **rest):
    n_in = len(args)

    def body(*refs):
        kernel(*refs[:n_in], *refs[n_in + len(after) :])

    return pl.pallas_call(
        body,
        grid_spec=pltpu.PrefetchScalarGridSpec(
            num_scalar_prefetch=scalars,
            grid=grid,
            in_specs=list(in_specs) + [ANYWHERE] * len(after),
            out_specs=out_specs,
            scratch_shapes=list(scratch),
        ),
        compiler_params=PARAMS,
        **rest,
    )(*args, *after)


def copy_rows(rows, table_ref, outs, held, sem):
    capacity = outs[0].shape[0]
    reads = [
        pltpu.make_async_copy(table_ref.at[row], held.at[c], sem.at[0, c])
        for c, row in enumerate(rows)
    ]
    writes = [
        pltpu.make_async_copy(held.at[c], outs[c // capacity].at[c % capacity], sem.at[1, c])
        for c in range(len(rows))
    ]
    for read in reads:
        read.start()

    def finish_copies():
        for read, write in zip(reads, writes):
            read.wait()
            write.start()
        for write in writes:
            write.wait()

    return finish_copies


def copies_of(table, count):
    return [
        pltpu.VMEM((count,) + table.shape[1:], table.dtype),
        pltpu.SemaphoreType.DMA((2, count)),
    ]


def request_kernel(capacity, n_dev, me_ref, row_ref, *rest):
    id_refs, table_ref = rest[:n_dev], rest[n_dev]
    outs, (plan_ref, held, sem) = rest[n_dev + 1 : -3], rest[-3:]
    n_seg = id_refs[0].shape[0]
    n_own = table_ref.shape[0]
    me = me_ref[0]
    spare = COLS - 1
    for c in range((n_dev - 1) * capacity):
        for row in (SEND, TERM, GIVEN):
            plan_ref[row, c] = 0 if row == SEND else -1
    for s in range(1, n_dev):
        slots = [row_ref[id_refs[s][k]] for k in range(n_seg)]
        order = jnp.int32(0)
        for slot in slots:
            mine = lax.div(slot, n_own) == me
            local = slot - me * n_own
            there = (n_dev - s - 1) * capacity + order
            plan_ref[SEND, jnp.where(mine, there, spare)] = local
            plan_ref[GIVEN, jnp.where(mine, (s - 1) * capacity + order, spare)] = local
            order = order + mine.astype(jnp.int32)
    rows = [plan_ref[SEND, c] for c in range(len(outs) * capacity)]
    finish_copies = copy_rows(rows, table_ref, outs, held, sem)
    slots = [row_ref[id_refs[0][k]] for k in range(n_seg)]
    owners = [lax.div(v, n_own) for v in slots]
    for k in range(n_seg):
        local = slots[k] - owners[k] * n_own
        order = jnp.int32(0)
        for q in range(k):
            order = order + (owners[q] == owners[k]).astype(jnp.int32)
        away = lax.rem(owners[k] - me + n_dev, n_dev)
        plan_ref[OWN, k] = jnp.where(away == 0, local, -1)
        from_owner = (n_dev - away - 1) * capacity + order
        plan_ref[SOURCE, k] = jnp.where(away == 0, local, n_own + from_owner)
        plan_ref[TERM, jnp.where(away == 0, spare, (away - 1) * capacity + order)] = k
    finish_copies()


def request(me, table_row, ids, table, capacity):
    n_dev = len(ids)
    count = n_dev - 1
    block = jax.ShapeDtypeStruct((capacity,) + table.shape[1:], table.dtype)
    *sends, plan = call(
        functools.partial(request_kernel, capacity, n_dev),
        (me.reshape(1), table_row, *ids, table),
        [SMEM] * (2 + n_dev) + [ANYWHERE],
        out_shape=[block] * count + [jax.ShapeDtypeStruct((8, COLS), jnp.int32)],
        out_specs=[HBM] * count + [SMEM],
        scratch=copies_of(table, count * capacity),
        cost_estimate=cost(0, table.size * 4),
        name="request",
    )
    return sends, plan


def rows_kernel(row, plan_ref, table_ref, *rest):
    outs, (held, sem) = rest[:-2], rest[-2:]
    rows = [jnp.maximum(plan_ref[row, c], 0) for c in range(len(outs) * outs[0].shape[0])]
    copy_rows(rows, table_ref, outs, held, sem)()


def rows_of(plan, row, table, count, capacity, after=()):
    block = jax.ShapeDtypeStruct((capacity,) + table.shape[1:], table.dtype)
    return call(
        functools.partial(rows_kernel, row),
        (plan, table),
        [SMEM, ANYWHERE],
        after,
        out_shape=[block] * count,
        out_specs=[HBM] * count,
        scratch=copies_of(table, count * capacity),
        cost_estimate=cost(0, table.size * 4),
        name="rows",
    )


def low_rank_kernel(plan_ref, act_ref, table_ref, *rest):
    blocks, (factor_ref, part_ref, sem) = rest[:-3], rest[-3:]
    n_own = table_ref.shape[0]
    n_seg, capacity = factor_ref.shape[0], blocks[0].shape[0]
    for k in range(n_seg):
        at = plan_ref[SOURCE, k]

        @pl.when(at < n_own)
        def _(k=k, at=at):
            pltpu.make_async_copy(table_ref.at[at], factor_ref.at[k], sem.at[k]).start()

        for n, ref in enumerate(blocks):
            slot = at - n_own - n * capacity

            @pl.when((slot >= 0) & (slot < capacity))
            def _(k=k, slot=slot, ref=ref):
                pltpu.make_async_copy(ref.at[slot], factor_ref.at[k], sem.at[k]).start()

    seg_rows = act_ref.shape[0] // n_seg
    for k in range(n_seg):
        pltpu.make_async_copy(table_ref.at[0], factor_ref.at[k], sem.at[k]).wait()
        part_ref[k] = lax.dot_general(
            factor_ref[k],
            act_ref[k * seg_rows : (k + 1) * seg_rows],
            (((1,), (1,)), ((), ())),
            preferred_element_type=F32,
        ).astype(part_ref.dtype)


def low_rank(plan, act, table, blocks, n_seg, after=()):
    _, rank, width = table.shape
    return call(
        low_rank_kernel,
        (plan, act, table, *blocks),
        [SMEM, VMEM] + [ANYWHERE] * (1 + len(blocks)),
        after,
        out_shape=[
            jax.ShapeDtypeStruct((n_seg, rank, width), BF16),
            jax.ShapeDtypeStruct((n_seg, rank, act.shape[0] // n_seg), BF16),
        ],
        out_specs=[VMEM, VMEM],
        scratch=[pltpu.SemaphoreType.DMA((n_seg,))],
        cost_estimate=cost(2 * act.size * rank, 4 * act.size),
        name="low_rank",
    )


def terms_kernel(live_ref, *rest):
    parts, (right_ref, act_ref, term_ref) = rest[:-3], rest[-3:]
    total = parts[0][0].astype(F32)
    for part in parts[1:]:
        total = total + part[0].astype(F32)
    column = lax.broadcasted_iota(jnp.int32, total.shape, 1)
    act = jnp.where(column < live_ref[pl.program_id(0)], total * SCALE, 0.0).astype(BF16)
    act_ref[0] = act
    term_ref[0] = jnp.dot(act, right_ref[...], preferred_element_type=F32).astype(BF16)


def make_terms(live_length, parts, right, after=()):
    n_seg, rank, seg_rows = parts[0].shape
    width = right.shape[1]
    small = pl.BlockSpec((1, rank, seg_rows), lambda k, *_: (k, 0, 0))
    return call(
        terms_kernel,
        (live_length, *parts, right),
        [small] * len(parts) + [pl.BlockSpec((seg_rows, width), lambda k, *_: (k, 0))],
        after,
        scalars=1,
        grid=(n_seg,),
        out_shape=[
            jax.ShapeDtypeStruct((n_seg, rank, seg_rows), BF16),
            jax.ShapeDtypeStruct((n_seg, rank, width), BF16),
        ],
        out_specs=[small, pl.BlockSpec((1, rank, width), lambda k, *_: (k, 0, 0))],
        cost_estimate=cost(2 * right.size * rank, 4 * right.size),
        name="terms",
    )


def total_kernel(plan_ref, terms_ref, *rest):
    blocks, out_ref = rest[:-1], rest[-1]
    capacity = blocks[0].shape[0]
    mine = pl.program_id(0)
    out_ref[...] = jnp.zeros_like(out_ref)
    sources = [(plan_ref[OWN, k], terms_ref, k) for k in range(terms_ref.shape[0])]
    for n, ref in enumerate(blocks):
        for j in range(capacity):
            sources.append((plan_ref[GIVEN, (n - 1) % len(blocks) * capacity + j], ref, j))
    for at, ref, k in sources:

        @pl.when(at == mine)
        def _(ref=ref, k=k):
            out_ref[0] += ref[k].astype(F32)


def totals(plan, terms, blocks, n_own, after=()):
    blocks = rotated(blocks)
    _, rank, width = terms.shape
    return call(
        total_kernel,
        (plan, terms, *blocks),
        [SMEM] + [VMEM] * (1 + len(blocks)),
        after,
        grid=(n_own,),
        out_shape=jax.ShapeDtypeStruct((n_own, rank, width), F32),
        out_specs=pl.BlockSpec((1, rank, width), lambda j: (j, 0, 0)),
        cost_estimate=cost(0, 4 * terms.size),
        name="totals",
    )


def segment_sum(act_ref, factor_ref):
    return jnp.concatenate(
        [
            lax.dot_general(
                act_ref[k], factor_ref[k], (((0,), (0,)), ((), ())), preferred_element_type=F32
            )
            for k in range(act_ref.shape[0])
        ],
        axis=0,
    )


def forward_kernel(x_ref, w_ref, out_ref):
    out_ref[...] = jnp.dot(x_ref[...], w_ref[...], preferred_element_type=F32).astype(out_ref.dtype)


def forward(x, weight, after=()):
    rows, width = x.shape
    full = weight.shape[1]
    return call(
        forward_kernel,
        (x, weight),
        [
            pl.BlockSpec((rows, width), lambda j: (0, 0)),
            pl.BlockSpec((width, TILE), lambda j: (0, j)),
        ],
        after,
        grid=(full // TILE,),
        out_shape=jax.ShapeDtypeStruct((rows, full), BF16),
        out_specs=pl.BlockSpec((rows, TILE), lambda j: (0, j)),
        cost_estimate=cost(2 * rows * width * full, 2 * width * full),
        name="forward",
    )


def rotated(blocks):
    return [blocks[-1], *blocks[:-1]]


def held_back(arrays, after):
    n = len(arrays)
    return call(
        lambda *refs: None,
        arrays,
        [ANYWHERE] * n,
        after,
        out_shape=[jax.ShapeDtypeStruct(x.shape, x.dtype) for x in arrays],
        out_specs=[ANYWHERE] * n,
        input_output_aliases={i: i for i in range(n)},
        cost_estimate=cost(0, 0),
        name="held_back",
    )


def backward_kernel(x_ref, w_ref, act_ref, factor_ref, out_ref):
    out = lax.dot_general(
        x_ref[...], w_ref[...], (((1,), (1,)), ((), ())), preferred_element_type=F32
    )
    out_ref[...] = (out + segment_sum(act_ref, factor_ref)).astype(out_ref.dtype)


def backward(x, weight, act, factors, after=()):
    rows, full = x.shape
    width = weight.shape[0]
    n_seg, rank, seg_rows = act.shape
    tile = min(256, width)
    return call(
        backward_kernel,
        (x, weight, act, factors),
        [
            pl.BlockSpec((rows, full), lambda j: (0, 0)),
            pl.BlockSpec((tile, full), lambda j: (j, 0)),
            pl.BlockSpec((n_seg, rank, seg_rows), lambda j: (0, 0, 0)),
            pl.BlockSpec((n_seg, rank, tile), lambda j: (0, 0, j)),
        ],
        after,
        grid=(width // tile,),
        out_shape=jax.ShapeDtypeStruct((rows, width), BF16),
        out_specs=pl.BlockSpec((rows, tile), lambda j: (0, j)),
        cost_estimate=cost(2 * rows * width * full, 2 * width * full),
        name="backward",
    )


def adapt_kernel(x_ref, act_ref, factor_ref, out_ref):
    out = x_ref[...].astype(F32) + segment_sum(act_ref, factor_ref)
    out_ref[...] = out.astype(out_ref.dtype)


def adapt(x, act, factors, after=()):
    rows, width = x.shape
    n_seg, rank, seg_rows = act.shape
    tile = min(512, width)
    here = pl.BlockSpec((rows, tile), lambda j: (0, j))
    return call(
        adapt_kernel,
        (x, act, factors),
        [
            here,
            pl.BlockSpec((n_seg, rank, seg_rows), lambda j: (0, 0, 0)),
            pl.BlockSpec((n_seg, rank, tile), lambda j: (0, 0, j)),
        ],
        after,
        grid=(width // tile,),
        out_shape=jax.ShapeDtypeStruct((rows, width), BF16),
        out_specs=here,
        cost_estimate=cost(2 * rows * width * rank, 4 * rows * width),
        name="adapt",
    )


def body(
    tokens,
    cotangent,
    weight,
    down_table,
    up_table,
    segment_adapter_id,
    segment_live_length,
    adapter_table_row,
):
    n_seg = segment_adapter_id.shape[0]
    n_own = down_table.shape[0]
    n_dev = lax.axis_size("dp")
    n_tensor = lax.axis_size("tensor")
    n_chips = n_tensor // 2
    capacity = max(2, n_seg // 2)

    def over_core(x):
        return lax.ppermute(x, "tensor", [(i, i ^ 1) for i in range(n_tensor)])

    def over_chips(x, s):
        pairs = [(i, (i // 2 + s) % n_chips * 2 + i % 2) for i in range(n_tensor)]
        return lax.ppermute(x, "tensor", pairs)

    def over_line(x, s):
        return lax.ppermute(x, "dp", [(i, (i + s) % n_dev) for i in range(n_dev)])

    shifts = range(1, n_dev)
    hops = range(1, n_chips)

    cot_rows = lax.all_gather(cotangent, "tensor", axis=1, tiled=True)

    ids = [segment_adapter_id] + [over_line(segment_adapter_id, s) for s in shifts]

    down_t = jnp.swapaxes(down_table, 1, 2)
    me_dev = lax.axis_index("dp").astype(jnp.int32)
    sends, plan = request(me_dev, adapter_table_row, ids, down_t, capacity)
    down_got = [over_line(x, s) for x, s in zip(sends, shifts)]

    sends = rows_of(plan, SEND, up_table, n_dev - 1, capacity, [sends[-1]])
    up_got = [over_line(x, s) for x, s in zip(sends, shifts)]

    (partial,) = held_back([forward(tokens, weight, [sends[-1]])], rotated(down_got))
    layer = lax.psum_scatter(partial, "tensor", scatter_dimension=1, tiled=True)

    def summed(part):
        part = (part.astype(F32) + over_core(part).astype(F32)).astype(BF16)
        return [part] + [over_chips(part, s) for s in hops]

    def give(terms, after):
        sends = rows_of(plan, TERM, terms, n_dev - 1, capacity)
        if after:
            sends = held_back(sends, rotated(after))
        return sends, [over_line(x, s) for x, s in zip(sends, shifts)]

    down_seg, part = low_rank(plan, tokens, down_t, down_got, n_seg, [partial])
    act, up_terms = make_terms(segment_live_length, summed(part), cotangent)

    sends, up_back = give(up_terms, ())
    up_seg, part = low_rank(plan, cotangent, up_table, up_got, n_seg, [sends[-1]])
    grad, down_terms = make_terms(segment_live_length, summed(part), tokens)

    sends, down_back = give(down_terms, up_back)
    up_grad = totals(plan, up_terms, up_back, n_own, [sends[-1]])
    token_input_gradient = backward(cot_rows, weight, grad, down_seg, [up_grad])
    layer_result = adapt(layer, act, up_seg, [token_input_gradient])
    down_grad = totals(plan, down_terms, down_back, n_own, [layer_result])
    return layer_result, token_input_gradient, jnp.swapaxes(down_grad, 1, 2), up_grad


def solution(mesh):
    placed = (
        P(("groups", "dp"), "tensor"),
        P(("groups", "dp"), "tensor"),
        P("tensor", None),
        P(("groups", "dp"), "tensor", None),
        P(("groups", "dp"), None, "tensor"),
        P(("groups", "dp")),
        P(("groups", "dp")),
        P("groups"),
    )
    return jax.shard_map(
        body,
        mesh=mesh,
        in_specs=placed,
        out_specs=(
            P(("groups", "dp"), "tensor"),
            P(("groups", "dp"), "tensor"),
            P(("groups", "dp"), "tensor", None),
            P(("groups", "dp"), None, "tensor"),
        ),
        check_vma=False,
    )
```

```python
import functools

import jax
import jax.numpy as jnp
from jax import lax
from jax.experimental import pallas as pl
from jax.experimental.pallas import tpu as pltpu
from jax.sharding import PartitionSpec as P

SCALE = 0.015625
COLS = 128
TILE = 512
SEND, SOURCE, TERM, GIVEN, OWN = range(5)
F32, BF16 = jnp.float32, jnp.bfloat16
SMEM = pl.BlockSpec(memory_space=pltpu.SMEM)
VMEM = pl.BlockSpec(memory_space=pltpu.VMEM)
ANYWHERE = pl.BlockSpec(memory_space=pl.ANY)
HBM = pl.BlockSpec(memory_space=pltpu.HBM)
PARAMS = pltpu.CompilerParams(vmem_limit_bytes=56 << 20)


def cost(flops, nbytes):
    return pl.CostEstimate(flops=flops, bytes_accessed=nbytes, transcendentals=0)


def call(kernel, args, in_specs, after=(), scalars=0, grid=(), out_specs=None, scratch=(), **rest):
    n_in = len(args)

    def body(*refs):
        kernel(*refs[:n_in], *refs[n_in + len(after) :])

    return pl.pallas_call(
        body,
        grid_spec=pltpu.PrefetchScalarGridSpec(
            num_scalar_prefetch=scalars,
            grid=grid,
            in_specs=list(in_specs) + [ANYWHERE] * len(after),
            out_specs=out_specs,
            scratch_shapes=list(scratch),
        ),
        compiler_params=PARAMS,
        **rest,
    )(*args, *after)


def copy_rows(rows, table_ref, outs, held, sem):
    capacity = outs[0].shape[0]
    reads = [
        pltpu.make_async_copy(table_ref.at[row], held.at[c], sem.at[0, c])
        for c, row in enumerate(rows)
    ]
    writes = [
        pltpu.make_async_copy(held.at[c], outs[c // capacity].at[c % capacity], sem.at[1, c])
        for c in range(len(rows))
    ]
    for read in reads:
        read.start()

    def pass_on():
        for read, write in zip(reads, writes):
            read.wait()
            write.start()

    def finish():
        for write in writes:
            write.wait()

    return pass_on, finish


def copies_of(table, count):
    return [
        pltpu.VMEM((count,) + table.shape[1:], table.dtype),
        pltpu.SemaphoreType.DMA((2, count)),
    ]


def request_kernel(capacity, n_dev, me_ref, row_ref, *rest):
    id_refs, table_ref = rest[:n_dev], rest[n_dev]
    outs, (plan_ref, held, sem) = rest[n_dev + 1 : -3], rest[-3:]
    n_seg = id_refs[0].shape[0]
    n_own = table_ref.shape[0]
    me = me_ref[0]
    spare = COLS - 1
    for c in range((n_dev - 1) * capacity):
        for row in (SEND, TERM, GIVEN):
            plan_ref[row, c] = 0 if row == SEND else -1
    for s in range(1, n_dev):
        slots = [row_ref[id_refs[s][k]] for k in range(n_seg)]
        order = jnp.int32(0)
        for slot in slots:
            mine = lax.div(slot, n_own) == me
            local = slot - me * n_own
            there = (n_dev - s - 1) * capacity + order
            plan_ref[SEND, jnp.where(mine, there, spare)] = local
            plan_ref[GIVEN, jnp.where(mine, (s - 1) * capacity + order, spare)] = local
            order = order + mine.astype(jnp.int32)
    rows = [plan_ref[SEND, c] for c in range(len(outs) * capacity)]
    pass_on, finish = copy_rows(rows, table_ref, outs, held, sem)
    pass_on()
    slots = [row_ref[id_refs[0][k]] for k in range(n_seg)]
    owners = [lax.div(v, n_own) for v in slots]
    for k in range(n_seg):
        local = slots[k] - owners[k] * n_own
        order = jnp.int32(0)
        for q in range(k):
            order = order + (owners[q] == owners[k]).astype(jnp.int32)
        away = lax.rem(owners[k] - me + n_dev, n_dev)
        plan_ref[OWN, k] = jnp.where(away == 0, local, -1)
        from_owner = (n_dev - away - 1) * capacity + order
        plan_ref[SOURCE, k] = jnp.where(away == 0, local, n_own + from_owner)
        plan_ref[TERM, jnp.where(away == 0, spare, (away - 1) * capacity + order)] = k
    finish()


def request(me, table_row, ids, table, capacity):
    n_dev = len(ids)
    count = n_dev - 1
    block = jax.ShapeDtypeStruct((capacity,) + table.shape[1:], table.dtype)
    *sends, plan = call(
        functools.partial(request_kernel, capacity, n_dev),
        (me.reshape(1), table_row, *ids, table),
        [SMEM] * (2 + n_dev) + [ANYWHERE],
        out_shape=[block] * count + [jax.ShapeDtypeStruct((8, COLS), jnp.int32)],
        out_specs=[HBM] * count + [SMEM],
        scratch=copies_of(table, count * capacity),
        cost_estimate=cost(0, table.size * 4),
        name="request",
    )
    return sends, plan


def rows_kernel(row, plan_ref, table_ref, *rest):
    outs, (held, sem) = rest[:-2], rest[-2:]
    rows = [jnp.maximum(plan_ref[row, c], 0) for c in range(len(outs) * outs[0].shape[0])]
    for step in copy_rows(rows, table_ref, outs, held, sem):
        step()


def rows_of(plan, row, table, count, capacity, after=()):
    block = jax.ShapeDtypeStruct((capacity,) + table.shape[1:], table.dtype)
    return call(
        functools.partial(rows_kernel, row),
        (plan, table),
        [SMEM, ANYWHERE],
        after,
        out_shape=[block] * count,
        out_specs=[HBM] * count,
        scratch=copies_of(table, count * capacity),
        cost_estimate=cost(0, table.size * 4),
        name="rows",
    )


def low_rank_kernel(plan_ref, act_ref, table_ref, *rest):
    blocks, (factor_ref, part_ref, sem) = rest[:-3], rest[-3:]
    n_own = table_ref.shape[0]
    n_seg, capacity = factor_ref.shape[0], blocks[0].shape[0]
    for k in range(n_seg):
        at = plan_ref[SOURCE, k]

        @pl.when(at < n_own)
        def _(k=k, at=at):
            pltpu.make_async_copy(table_ref.at[at], factor_ref.at[k], sem.at[k]).start()

        for n, ref in enumerate(blocks):
            slot = at - n_own - n * capacity

            @pl.when((slot >= 0) & (slot < capacity))
            def _(k=k, slot=slot, ref=ref):
                pltpu.make_async_copy(ref.at[slot], factor_ref.at[k], sem.at[k]).start()

    seg_rows = act_ref.shape[0] // n_seg
    for k in range(n_seg):
        pltpu.make_async_copy(table_ref.at[0], factor_ref.at[k], sem.at[k]).wait()
        part_ref[k] = lax.dot_general(
            factor_ref[k],
            act_ref[k * seg_rows : (k + 1) * seg_rows],
            (((1,), (1,)), ((), ())),
            preferred_element_type=F32,
        ).astype(part_ref.dtype)


def low_rank(plan, act, table, blocks, n_seg, after=()):
    _, rank, width = table.shape
    return call(
        low_rank_kernel,
        (plan, act, table, *blocks),
        [SMEM, VMEM] + [ANYWHERE] * (1 + len(blocks)),
        after,
        out_shape=[
            jax.ShapeDtypeStruct((n_seg, rank, width), BF16),
            jax.ShapeDtypeStruct((n_seg, rank, act.shape[0] // n_seg), BF16),
        ],
        out_specs=[VMEM, VMEM],
        scratch=[pltpu.SemaphoreType.DMA((n_seg,))],
        cost_estimate=cost(2 * act.size * rank, 4 * act.size),
        name="low_rank",
    )


def terms_kernel(live_ref, *rest):
    parts, (right_ref, act_ref, term_ref) = rest[:-3], rest[-3:]
    total = parts[0][0].astype(F32)
    for part in parts[1:]:
        total = total + part[0].astype(F32)
    column = lax.broadcasted_iota(jnp.int32, total.shape, 1)
    act = jnp.where(column < live_ref[pl.program_id(0)], total * SCALE, 0.0).astype(BF16)
    act_ref[0] = act
    term_ref[0] = jnp.dot(act, right_ref[...], preferred_element_type=F32).astype(BF16)


def make_terms(live_length, parts, right, after=()):
    n_seg, rank, seg_rows = parts[0].shape
    width = right.shape[1]
    small = pl.BlockSpec((1, rank, seg_rows), lambda k, *_: (k, 0, 0))
    return call(
        terms_kernel,
        (live_length, *parts, right),
        [small] * len(parts) + [pl.BlockSpec((seg_rows, width), lambda k, *_: (k, 0))],
        after,
        scalars=1,
        grid=(n_seg,),
        out_shape=[
            jax.ShapeDtypeStruct((n_seg, rank, seg_rows), BF16),
            jax.ShapeDtypeStruct((n_seg, rank, width), BF16),
        ],
        out_specs=[small, pl.BlockSpec((1, rank, width), lambda k, *_: (k, 0, 0))],
        cost_estimate=cost(2 * right.size * rank, 4 * right.size),
        name="terms",
    )


def total_kernel(plan_ref, terms_ref, *rest):
    blocks, out_ref = rest[:-1], rest[-1]
    capacity = blocks[0].shape[0]
    mine = pl.program_id(0)
    out_ref[...] = jnp.zeros_like(out_ref)
    sources = [(plan_ref[OWN, k], terms_ref, k) for k in range(terms_ref.shape[0])]
    for n, ref in enumerate(blocks):
        for j in range(capacity):
            sources.append((plan_ref[GIVEN, (n - 1) % len(blocks) * capacity + j], ref, j))
    for at, ref, k in sources:

        @pl.when(at == mine)
        def _(ref=ref, k=k):
            out_ref[0] += ref[k].astype(F32)


def totals(plan, terms, blocks, n_own, after=()):
    blocks = rotated(blocks)
    _, rank, width = terms.shape
    return call(
        total_kernel,
        (plan, terms, *blocks),
        [SMEM] + [VMEM] * (1 + len(blocks)),
        after,
        grid=(n_own,),
        out_shape=jax.ShapeDtypeStruct((n_own, rank, width), F32),
        out_specs=pl.BlockSpec((1, rank, width), lambda j: (j, 0, 0)),
        cost_estimate=cost(0, 4 * terms.size),
        name="totals",
    )


def segment_sum(act_ref, factor_ref):
    return jnp.concatenate(
        [
            lax.dot_general(
                act_ref[k], factor_ref[k], (((0,), (0,)), ((), ())), preferred_element_type=F32
            )
            for k in range(act_ref.shape[0])
        ],
        axis=0,
    )


def forward_kernel(x_ref, w_ref, out_ref):
    out_ref[...] = jnp.dot(x_ref[...], w_ref[...], preferred_element_type=F32).astype(out_ref.dtype)


def forward(x, weight, after=()):
    rows, width = x.shape
    full = weight.shape[1]
    return call(
        forward_kernel,
        (x, weight),
        [
            pl.BlockSpec((rows, width), lambda j: (0, 0)),
            pl.BlockSpec((width, TILE), lambda j: (0, j)),
        ],
        after,
        grid=(full // TILE,),
        out_shape=jax.ShapeDtypeStruct((rows, full), BF16),
        out_specs=pl.BlockSpec((rows, TILE), lambda j: (0, j)),
        cost_estimate=cost(2 * rows * width * full, 2 * width * full),
        name="forward",
    )


def rotated(blocks):
    return [blocks[-1], *blocks[:-1]]


def held_back(arrays, after):
    n = len(arrays)
    return call(
        lambda *refs: None,
        arrays,
        [ANYWHERE] * n,
        after,
        out_shape=[jax.ShapeDtypeStruct(x.shape, x.dtype) for x in arrays],
        out_specs=[ANYWHERE] * n,
        input_output_aliases={i: i for i in range(n)},
        cost_estimate=cost(0, 0),
        name="held_back",
    )


def backward_kernel(x_ref, w_ref, act_ref, factor_ref, out_ref):
    out = lax.dot_general(
        x_ref[...], w_ref[...], (((1,), (1,)), ((), ())), preferred_element_type=F32
    )
    out_ref[...] = (out + segment_sum(act_ref, factor_ref)).astype(out_ref.dtype)


def backward(x, weight, act, factors, after=()):
    rows, full = x.shape
    width = weight.shape[0]
    n_seg, rank, seg_rows = act.shape
    tile = min(256, width)
    return call(
        backward_kernel,
        (x, weight, act, factors),
        [
            pl.BlockSpec((rows, full), lambda j: (0, 0)),
            pl.BlockSpec((tile, full), lambda j: (j, 0)),
            pl.BlockSpec((n_seg, rank, seg_rows), lambda j: (0, 0, 0)),
            pl.BlockSpec((n_seg, rank, tile), lambda j: (0, 0, j)),
        ],
        after,
        grid=(width // tile,),
        out_shape=jax.ShapeDtypeStruct((rows, width), BF16),
        out_specs=pl.BlockSpec((rows, tile), lambda j: (0, j)),
        cost_estimate=cost(2 * rows * width * full, 2 * width * full),
        name="backward",
    )


def adapt_kernel(x_ref, act_ref, factor_ref, out_ref):
    out = x_ref[...].astype(F32) + segment_sum(act_ref, factor_ref)
    out_ref[...] = out.astype(out_ref.dtype)


def adapt(x, act, factors, after=()):
    rows, width = x.shape
    n_seg, rank, seg_rows = act.shape
    tile = min(512, width)
    here = pl.BlockSpec((rows, tile), lambda j: (0, j))
    return call(
        adapt_kernel,
        (x, act, factors),
        [
            here,
            pl.BlockSpec((n_seg, rank, seg_rows), lambda j: (0, 0, 0)),
            pl.BlockSpec((n_seg, rank, tile), lambda j: (0, 0, j)),
        ],
        after,
        grid=(width // tile,),
        out_shape=jax.ShapeDtypeStruct((rows, width), BF16),
        out_specs=here,
        cost_estimate=cost(2 * rows * width * rank, 4 * rows * width),
        name="adapt",
    )


def body(
    tokens,
    cotangent,
    weight,
    down_table,
    up_table,
    segment_adapter_id,
    segment_live_length,
    adapter_table_row,
):
    n_seg = segment_adapter_id.shape[0]
    n_own = down_table.shape[0]
    n_dev = lax.axis_size("dp")
    n_tensor = lax.axis_size("tensor")
    n_chips = n_tensor // 2
    capacity = max(2, n_seg // 2)

    def over_core(x):
        return lax.ppermute(x, "tensor", [(i, i ^ 1) for i in range(n_tensor)])

    def over_chips(x, s):
        pairs = [(i, (i // 2 + s) % n_chips * 2 + i % 2) for i in range(n_tensor)]
        return lax.ppermute(x, "tensor", pairs)

    def over_line(x, s):
        return lax.ppermute(x, "dp", [(i, (i + s) % n_dev) for i in range(n_dev)])

    shifts = range(1, n_dev)
    hops = range(1, n_chips)

    cot_rows = lax.all_gather(cotangent, "tensor", axis=1, tiled=True)

    ids = [segment_adapter_id] + [over_line(segment_adapter_id, s) for s in shifts]

    down_t = jnp.swapaxes(down_table, 1, 2)
    me_dev = lax.axis_index("dp").astype(jnp.int32)
    sends, plan = request(me_dev, adapter_table_row, ids, down_t, capacity)
    down_got = [over_line(x, s) for x, s in zip(sends, shifts)]

    sends = rows_of(plan, SEND, up_table, n_dev - 1, capacity, [sends[-1]])
    up_got = [over_line(x, s) for x, s in zip(sends, shifts)]

    (partial,) = held_back([forward(tokens, weight, [sends[-1]])], rotated(down_got))
    layer = lax.psum_scatter(partial, "tensor", scatter_dimension=1, tiled=True)

    def summed(part):
        part = (part.astype(F32) + over_core(part).astype(F32)).astype(BF16)
        return [part] + [over_chips(part, s) for s in hops]

    def give(terms, after):
        sends = rows_of(plan, TERM, terms, n_dev - 1, capacity)
        if after:
            sends = held_back(sends, rotated(after))
        return sends, [over_line(x, s) for x, s in zip(sends, shifts)]

    down_seg, part = low_rank(plan, tokens, down_t, down_got, n_seg, [partial])
    act, up_terms = make_terms(segment_live_length, summed(part), cotangent)

    sends, up_back = give(up_terms, ())
    up_seg, part = low_rank(plan, cotangent, up_table, up_got, n_seg, [sends[-1]])
    grad, down_terms = make_terms(segment_live_length, summed(part), tokens)

    sends, down_back = give(down_terms, up_back)
    up_grad = totals(plan, up_terms, up_back, n_own, [sends[-1]])
    token_input_gradient = backward(cot_rows, weight, grad, down_seg, [up_grad])
    layer_result = adapt(layer, act, up_seg, [token_input_gradient])
    down_grad = totals(plan, down_terms, down_back, n_own, [layer_result])
    return layer_result, token_input_gradient, jnp.swapaxes(down_grad, 1, 2), up_grad


def solution(mesh):
    placed = (
        P(("groups", "dp"), "tensor"),
        P(("groups", "dp"), "tensor"),
        P("tensor", None),
        P(("groups", "dp"), "tensor", None),
        P(("groups", "dp"), None, "tensor"),
        P(("groups", "dp")),
        P(("groups", "dp")),
        P("groups"),
    )
    return jax.shard_map(
        body,
        mesh=mesh,
        in_specs=placed,
        out_specs=(
            P(("groups", "dp"), "tensor"),
            P(("groups", "dp"), "tensor"),
            P(("groups", "dp"), "tensor", None),
            P(("groups", "dp"), None, "tensor"),
        ),
        check_vma=False,
    )
```
